32 devices in a mesh: grp: 4 (over y, x), dev: 8 (over z, core).
Axes of the slice: x: 2, y: 2, z: 4, core: 2. Of those that a mesh axis runs over, the one named last changes fastest.
Arguments:
- boundary_heat_flux: float32 [4096, 4096], P('grp', 'dev'), may hold values from -6 to 6
- layer_kernel: float32 [2, 2, 2048, 4096], P(None, None, ('grp', 'dev')), may hold values from -6 to 6
Outputs:
- thermal_rise: float32 [2, 4096, 4096], P(None, 'grp', 'dev')
The draws below stay inside these ranges and needn't reach their ends.
All inputs are finite; a program needn't handle non-finite values.
Results may differ from the reference program's by a relative error of at most 0.0001.
Values sent between devices are 32-bit elements; how exact they have to be, the bound alone decides.
A program may use at most 128 MiB of HBM per device.

```python
import jax
import jax.numpy as jnp

NX = 4096
NY = 4096
LAYERS = 2


def level_of(own_key, shape, cuts, least, high):
    loudness = 1.0
    for dim, shards_of in cuts:
        steps = jax.random.uniform(jax.random.fold_in(jax.random.fold_in(own_key, 6), dim), (shards_of,), jnp.float32, least / len(cuts), high / len(cuts))
        loudness = loudness * jnp.repeat(jnp.exp(steps), shape[dim] // shards_of).reshape((-1,) + (1,) * (len(shape) - 1 - dim))
    return loudness


def gaussian(key, shape, spread, limit, split=(), held_as=jnp.bfloat16):
    loudness = level_of(key, shape, split, -0.22, 0.18) if split else 1.0
    result = jax.random.normal(key, shape, jnp.float32) * spread * loudness
    return jnp.minimum(jnp.maximum(result, -limit), limit).astype(held_as)


def setup_inputs(seed: int = 0) -> dict:
    seeds = jax.random.split(jax.random.key(seed), 3)
    return {
        "boundary_heat_flux": gaussian(seeds[0], (NX, NY), 1.0, 6.0, ((0, 4), (1, 8)), jnp.float32),
        "layer_kernel": gaussian(seeds[1], (LAYERS, 2, NY // 2, NX), 1.0, 6.0, ((2, 32),), jnp.float32),
    }


def full_transfer(kernel_pair):
    lower = kernel_pair[0] + 1j * kernel_pair[1]
    mirrored = jnp.roll(jnp.flip(lower, 1), 1, 1)
    upper = jnp.conj(jnp.flip(mirrored[1:], 0))
    middle = jnp.zeros((1, lower.shape[1]), lower.dtype)
    return jnp.concatenate([lower, middle, upper], axis=0).T


def reference(boundary_heat_flux, layer_kernel):
    spectrum = jnp.fft.fft2(boundary_heat_flux)
    outputs = []
    for layer_pos in range(LAYERS):
        transfer = full_transfer(layer_kernel[layer_pos])
        field = jnp.fft.ifft2(spectrum * transfer)
        outputs.append(jnp.real(field).astype(jnp.float32))
    return jnp.stack(outputs)
```

```python
import functools
import math

import jax
import jax.numpy as jnp
import numpy as np
from jax import lax
from jax.experimental import pallas as pl
from jax.experimental.pallas import tpu as pltpu
from jax.sharding import PartitionSpec as P


def split_length(length):
    leading = 1
    for candidate in range(1, math.isqrt(length) + 1):
        if length % candidate == 0 and candidate % 2 == 0:
            leading = candidate
    return (leading, length // leading)


def tables(leading, trailing, direction):
    length = leading * trailing
    outer_idx = lax.iota(jnp.int32, leading)
    inner_idx = lax.iota(jnp.int32, trailing)
    angle_outer = (outer_idx[:, None] * outer_idx[None, :] % leading).astype(jnp.float32) * (
        2.0 * math.pi / leading
    )
    angle_twist = (outer_idx[:, None] * inner_idx[None, :] % length).astype(jnp.float32) * (
        2.0 * math.pi / length
    )
    angle_inner = (inner_idx[:, None] * inner_idx[None, :] % trailing).astype(jnp.float32) * (
        2.0 * math.pi / trailing
    )
    return (
        jnp.cos(angle_outer),
        direction * jnp.sin(angle_outer),
        jnp.cos(angle_twist),
        direction * jnp.sin(angle_twist),
        jnp.cos(angle_inner),
        direction * jnp.sin(angle_inner),
    )


def contract(pattern, table, values):
    return jnp.einsum(
        pattern, table, values, precision=lax.Precision.HIGHEST, preferred_element_type=jnp.float32
    )


def section_outer(real_in, imag_in, table, pattern):
    cos_outer, sin_outer, cos_twist, sin_twist = (table[0], table[1], table[2], table[3])
    if imag_in is None:
        real_mid = contract(pattern, cos_outer, real_in)
        imag_mid = contract(pattern, sin_outer, real_in)
    else:
        real_mid = contract(pattern, cos_outer, real_in) - contract(pattern, sin_outer, imag_in)
        imag_mid = contract(pattern, cos_outer, imag_in) + contract(pattern, sin_outer, real_in)
    return (
        real_mid * cos_twist - imag_mid * sin_twist,
        imag_mid * cos_twist + real_mid * sin_twist,
    )


def section_inner(real_mid, imag_mid, table, pattern, real_only):
    cos_inner, sin_inner = (table[4], table[5])
    real_out = contract(pattern, cos_inner, real_mid) - contract(pattern, sin_inner, imag_mid)
    if real_only:
        return real_out
    imag_out = contract(pattern, cos_inner, imag_mid) + contract(pattern, sin_inner, real_mid)
    return (real_out, imag_out)


def reflect_first(values):
    return jnp.roll(jnp.flip(values, -1), 1, -1)


def into_frequency(real_part, imag_part):
    return (
        lax.all_to_all(
            lax.all_to_all(real_part, "grp", split_axis=0, concat_axis=3, tiled=True),
            "dev",
            split_axis=1,
            concat_axis=4,
            tiled=True,
        ),
        lax.all_to_all(
            lax.all_to_all(imag_part, "grp", split_axis=0, concat_axis=3, tiled=True),
            "dev",
            split_axis=1,
            concat_axis=4,
            tiled=True,
        ),
    )


def to_spatial(real_part, imag_part):
    return (
        lax.all_to_all(
            lax.all_to_all(real_part, "grp", split_axis=4, concat_axis=1, tiled=True),
            "dev",
            split_axis=5,
            concat_axis=2,
            tiled=True,
        ),
        lax.all_to_all(
            lax.all_to_all(imag_part, "grp", split_axis=4, concat_axis=1, tiled=True),
            "dev",
            split_axis=5,
            concat_axis=2,
            tiled=True,
        ),
    )


def body(boundary_heat_flux, layer_kernel):
    groups = lax.axis_size("grp")
    members = lax.axis_size("dev")
    columns = lax.all_to_all(boundary_heat_flux, "dev", split_axis=0, concat_axis=1, tiled=True)
    x_rows = columns.shape[0]
    width_y = columns.shape[1]
    width_x = groups * members * x_rows
    half_y = width_y // 2
    block_rows = half_y // (groups * members)
    lead_y, trail_y = split_length(width_y)
    leading_horizontal, trail_x = split_length(width_x)
    ahead_vertical = tables(lead_y, trail_y, -1.0)
    forward_x = tables(leading_horizontal, trail_x, -1.0)
    backward_x = tables(leading_horizontal, trail_x, 1.0)
    backward_y = tables(lead_y, trail_y, 1.0)
    device_pos = lax.axis_index("grp") * members + lax.axis_index("dev")
    first_row = jnp.logical_and(device_pos == 0, lax.iota(jnp.int32, block_rows) == 0)
    first_row = first_row.astype(jnp.float32)[:, None]
    real_mid, imag_mid = section_outer(
        columns.reshape(x_rows, lead_y, trail_y), None, ahead_vertical, "ap,rpq->raq"
    )
    real_spec, imag_spec = section_inner(real_mid, imag_mid, ahead_vertical, "bq,raq->bar", False)
    real_spec = real_spec.reshape(width_y, x_rows)
    imag_spec = imag_spec.reshape(width_y, x_rows)
    lower_shape = (groups, members, block_rows, x_rows)
    sides = 2
    real_remainder = jnp.roll(jnp.flip(real_spec, 0), 1, 0)[:half_y]
    imag_tail = jnp.roll(jnp.flip(imag_spec, 0), 1, 0)[:half_y]
    real_send = jnp.stack(
        [real_spec[:half_y].reshape(lower_shape), real_remainder.reshape(lower_shape)], axis=2
    )
    imag_send = jnp.stack(
        [imag_spec[:half_y].reshape(lower_shape), imag_tail.reshape(lower_shape)], axis=2
    )
    local_rows = sides * block_rows
    shape_sent = (groups, members, local_rows, 1, 1, x_rows)
    real_recv, imag_recv = into_frequency(
        real_send.reshape(shape_sent), imag_send.reshape(shape_sent)
    )
    real_mid, imag_mid = section_outer(
        real_recv.reshape(local_rows, leading_horizontal, trail_x),
        imag_recv.reshape(local_rows, leading_horizontal, trail_x),
        forward_x,
        "ap,rpq->raq",
    )
    real_freq, imag_freq = section_inner(real_mid, imag_mid, forward_x, "bq,raq->rba", False)
    real_freq = real_freq.reshape(local_rows, width_x)
    imag_freq = imag_freq.reshape(local_rows, width_x)
    norm_factor = 1.0 / (width_x * width_y)

    def inverse_x(kernel_pair):
        kernel_real = kernel_pair[0]
        kernel_imag = kernel_pair[1]
        keep_rows = 1.0 - first_row
        kernel_real = jnp.concatenate([kernel_real, reflect_first(kernel_real) * keep_rows], axis=0)
        kernel_imag = jnp.concatenate(
            [kernel_imag, -reflect_first(kernel_imag) * keep_rows], axis=0
        )
        real_prod = real_freq * kernel_real - imag_freq * kernel_imag
        imag_prod = real_freq * kernel_imag + imag_freq * kernel_real
        central_couple = section_outer(
            real_prod.reshape(local_rows, leading_horizontal, trail_x),
            imag_prod.reshape(local_rows, leading_horizontal, trail_x),
            backward_x,
            "ap,rpq->raq",
        )
        real_out, imag_out = section_inner(
            central_couple[0], central_couple[1], backward_x, "bq,raq->rba", False
        )
        real_out = real_out.reshape(local_rows, width_x)
        imag_out = imag_out.reshape(local_rows, width_x)
        shape_back = (1, 1, local_rows, groups, members, x_rows)
        return (real_out.reshape(shape_back), imag_out.reshape(shape_back))

    def inverse_y(real_part, imag_part):
        zero_row = jnp.zeros((1, x_rows), jnp.float32)

        def arrange(values):
            paired = values.reshape(groups * members, 2, block_rows, x_rows)
            lower = paired[:, 0].reshape(half_y, x_rows)
            upper = paired[:, 1].reshape(half_y, x_rows)
            return jnp.concatenate([lower, zero_row, jnp.flip(upper[1:], 0)], axis=0)

        central_couple = section_outer(
            arrange(real_part).reshape(lead_y, trail_y, x_rows),
            arrange(imag_part).reshape(lead_y, trail_y, x_rows),
            backward_y,
            "ap,pqr->raq",
        )
        real_out = section_inner(
            central_couple[0], central_couple[1], backward_y, "bq,raq->rba", True
        )
        return real_out.reshape(x_rows, width_y) * norm_factor

    def finish(kernels):
        real_back, imag_back = jax.vmap(inverse_x)(kernels)
        real_part, imag_part = to_spatial(real_back, imag_back)
        rows_done = jax.vmap(inverse_y)(real_part, imag_part)
        return lax.all_to_all(rows_done, "dev", split_axis=2, concat_axis=1, tiled=True)

    thermal_rise = jnp.concatenate(
        [
            finish(layer_kernel[layer_pos : layer_pos + 1])
            for layer_pos in range(layer_kernel.shape[0])
        ],
        axis=0,
    )
    return thermal_rise


MESH = pl.DeviceIdType.MESH
RADIX = 8
LANES = 128
VMEM_LIMIT = 56 * 1024 * 1024
HALF_ROOT = math.sqrt(0.5)


def high_low(values):
    high = values.astype(jnp.bfloat16)
    return high, (values - high.astype(jnp.float32)).astype(jnp.bfloat16)


def split_table(table):
    table = np.asarray(table, np.float32)
    high = table.astype(jnp.bfloat16)
    low = (table - high.astype(np.float32)).astype(jnp.bfloat16)
    return jnp.asarray(np.stack([high, low]))


def complex_table(rows, columns, length, direction):
    angle = (np.outer(np.arange(rows), np.arange(columns)) % length) * (2.0 * np.pi / length)
    cos, sin = np.cos(angle), direction * np.sin(angle)
    return np.concatenate(
        [np.concatenate([cos, sin], axis=1), np.concatenate([-sin, cos], axis=1)], axis=0
    )


def twiddle_table(points, length, direction):
    angle = (np.outer(np.arange(RADIX), np.arange(points)) % length) * (2.0 * np.pi / length)
    return jnp.asarray(
        np.stack([np.cos(angle), direction * np.sin(angle)], axis=1).astype(np.float32)
    )


def add(a, b):
    return (a[0] + b[0], a[1] + b[1])


def sub(a, b):
    return (a[0] - b[0], a[1] - b[1])


def times(a, b):
    return (a[0] * b[0] - a[1] * b[1], a[0] * b[1] + a[1] * b[0])


def quarter(a, direction):
    return (-a[1], a[0]) if direction > 0 else (a[1], -a[0])


def eighth(a, direction):
    if direction > 0:
        return ((a[0] - a[1]) * HALF_ROOT, (a[0] + a[1]) * HALF_ROOT)
    return ((a[0] + a[1]) * HALF_ROOT, (a[1] - a[0]) * HALF_ROOT)


def four_point(a, direction):
    e0, e1 = add(a[0], a[2]), sub(a[0], a[2])
    o0, o1 = add(a[1], a[3]), quarter(sub(a[1], a[3]), direction)
    return [add(e0, o0), add(e1, o1), sub(e0, o0), sub(e1, o1)]


def eight_point(a, direction):
    even = four_point(a[0::2], direction)
    odd = four_point(a[1::2], direction)
    odd = [
        odd[0],
        eighth(odd[1], direction),
        quarter(odd[2], direction),
        quarter(eighth(odd[3], direction), direction),
    ]
    return [add(e, o) for e, o in zip(even, odd)] + [sub(e, o) for e, o in zip(even, odd)]


def eight_point_of_real(a):
    s0, d0 = a[0] + a[4], a[0] - a[4]
    s1, d1 = a[1] + a[5], a[1] - a[5]
    s2, d2 = a[2] + a[6], a[2] - a[6]
    s3, d3 = a[3] + a[7], a[3] - a[7]
    p, q = (d1 - d3) * HALF_ROOT, (d1 + d3) * HALF_ROOT
    zero = jnp.zeros_like(s0)
    x1 = (d0 + p, -d2 - q)
    x3 = (d0 - p, d2 - q)
    x2 = (s0 - s2, s3 - s1)
    ev, od = s0 + s2, s1 + s3
    conj = lambda z: (z[0], -z[1])
    return [(ev + od, zero), x1, x2, x3, (ev - od, zero), conj(x3), conj(x2), conj(x1)]


def eight_point_to_real(b):
    c1, c2, c3 = [(b[i][0] + b[8 - i][0], b[i][1] - b[8 - i][1]) for i in (1, 2, 3)]
    p, m = b[0][0] + b[4][0], b[0][0] - b[4][0]
    e0, e2 = p + c2[0], p - c2[0]
    e1, e3 = m - c2[1], m + c2[1]
    o0 = c1[0] + c3[0]
    o2 = c3[1] - c1[1]
    o1 = (c1[0] - c1[1] - c3[0] - c3[1]) * HALF_ROOT
    o3 = (c3[0] - c3[1] - c1[0] - c1[1]) * HALF_ROOT
    return [e0 + o0, e1 + o1, e2 + o2, e3 + o3, e0 - o0, e1 - o1, e2 - o2, e3 - o3]


def three_products(high, low, table_high, table_low):
    dot = functools.partial(jnp.dot, preferred_element_type=jnp.float32)
    return dot(high, table_high) + dot(high, table_low) + dot(low, table_high)


def exchange_kernel(counts, whole, src, dst, send_sem, recv_sem, own_sem):
    groups, members = counts
    grp, dev = lax.axis_index("grp"), lax.axis_index("dev")
    count = groups * members if whole else members
    me = grp * members + dev if whole else dev

    def place(pos):
        return (pos // members, pos % members) if whole else (grp, pos)

    barrier = pltpu.get_barrier_semaphore()
    for offset in range(1, count):
        pl.semaphore_signal(
            barrier, inc=1, device_id=place((me + offset) % count), device_id_type=MESH
        )
    pl.semaphore_wait(barrier, count - 1)

    def copy(offset, source, target):
        return pltpu.make_async_remote_copy(
            src_ref=src.at[target],
            dst_ref=dst.at[source],
            send_sem=send_sem.at[offset],
            recv_sem=recv_sem.at[offset],
            device_id=place(target),
            device_id_type=MESH,
        )

    for offset in range(1, count):
        copy(offset, me, (me + offset) % count).start()
    own = pltpu.make_async_copy(src.at[me], dst.at[me], own_sem)
    own.start()
    own.wait()
    for offset in range(1, count):
        copy(offset, me, (me + offset) % count).wait_send()
        copy(offset, (me + count - offset) % count, (me + offset) % count).wait_recv()


def exchange(values, counts, whole, collective_id):
    count = values.shape[0]
    return pl.pallas_call(
        functools.partial(exchange_kernel, counts, whole),
        out_shape=jax.ShapeDtypeStruct(values.shape, values.dtype),
        in_specs=[pl.BlockSpec(memory_space=pl.ANY)],
        out_specs=pl.BlockSpec(memory_space=pl.ANY),
        scratch_shapes=[
            pltpu.SemaphoreType.DMA((count,)),
            pltpu.SemaphoreType.DMA((count,)),
            pltpu.SemaphoreType.DMA,
        ],
        compiler_params=pltpu.CompilerParams(collective_id=collective_id, has_side_effects=True),
    )(values)


def forward_y_kernel(flux, table, twiddle, out, high, low):
    members, x_rows, trail = flux.shape
    count, _, block_rows, _ = out.shape
    sub_rows = block_rows // RADIX

    @pl.loop(0, x_rows // 16)
    def _(chunk):
        rows = pl.ds(pl.multiple_of(chunk * 16, 16), 16)
        for lane in range(trail // LANES):
            lanes = slice(lane * LANES, (lane + 1) * LANES)
            parts = eight_point_of_real([flux[s, rows, lanes] for s in range(RADIX)])
            for v0 in range(RADIX):
                real, imag = times(
                    parts[v0], (twiddle[v0, 0:1, lanes], twiddle[v0, 1:2, lanes])
                )
                for part, value in enumerate((real, imag)):
                    to = slice(part * trail + lane * LANES, part * trail + (lane + 1) * LANES)
                    hi, lo = high_low(value)
                    high[v0, rows, to] = hi
                    low[v0, rows, to] = lo

    @pl.loop(0, RADIX // 2)
    def _(pair):
        hi = high[pl.ds(pair * 2, 2)].reshape(2 * x_rows, 2 * trail)
        lo = low[pl.ds(pair * 2, 2)].reshape(2 * x_rows, 2 * trail)

        def dot(a, b):
            return lax.dot_general(
                a, b, (((1,), (1,)), ((), ())), preferred_element_type=jnp.float32
            )

        half = table.shape[1] // 2
        for part in range(2):
            t_hi = table[0, part * half : (part + 1) * half]
            t_lo = table[1, part * half : (part + 1) * half]
            result = dot(t_hi, hi) + dot(t_lo, hi) + dot(t_hi, lo)
            for side in range(2):
                piece = result[:, side * x_rows : (side + 1) * x_rows]
                piece = piece.reshape(count, sub_rows, x_rows)
                for k in range(count):
                    out[k, part, pl.ds(pair * 2 + side, sub_rows, stride=RADIX), :] = piece[k]


def middle_kernel(recv, kernel_ref, weight, table_in, table_out, twiddle, out, hi_a, lo_a, mid, hi_b, lo_b):
    count, _, block_rows, x_rows = recv.shape
    layers = kernel_ref.shape[0]
    groups = count // RADIX
    points = groups * x_rows
    rows_all = RADIX * block_rows

    @pl.loop(0, RADIX)
    def _(d):
        for g in range(groups):
            for part in range(2):
                to = slice(part * points + g * x_rows, part * points + (g + 1) * x_rows)
                hi, lo = high_low(recv[g * RADIX + d, part])
                hi_a[d, :, to] = hi
                lo_a[d, :, to] = lo

    tiles, _, width = table_in.shape[1:]

    @pl.loop(0, tiles)
    def _(n):
        result = three_products(
            hi_a[...].reshape(rows_all, 2 * points),
            lo_a[...].reshape(rows_all, 2 * points),
            table_in[0, n],
            table_in[1, n],
        )
        mid[n] = result.reshape(RADIX, block_rows, width)

    @pl.loop(0, block_rows // 16)
    def _(chunk):
        rows = pl.ds(pl.multiple_of(chunk * 16, 16), 16)
        scale = weight[rows, :]
        for lane in range(points // LANES):
            column = lane * LANES
            lanes = slice(column, column + LANES)
            within = slice(column % width, column % width + LANES)
            tile = column // width
            turn = [(twiddle[d, 0:1, lanes], twiddle[d, 1:2, lanes]) for d in range(RADIX)]
            spec = eight_point(
                [
                    times(
                        (mid[tile, d, rows, within], mid[tile + tiles // 2, d, rows, within]),
                        turn[d],
                    )
                    for d in range(RADIX)
                ],
                -1.0,
            )
            spec = [(a * scale, b * scale) for a, b in spec]
            for layer in range(layers):
                prod = []
                for u2 in range(RADIX):
                    at = slice(u2 * points + column, u2 * points + column + LANES)
                    prod.append(
                        times(spec[u2], (kernel_ref[layer, 0, rows, at], kernel_ref[layer, 1, rows, at]))
                    )
                back = eight_point(prod, 1.0)
                for d in range(RADIX):
                    both = times(back[d], (turn[d][0], -turn[d][1]))
                    for part in range(2):
                        to = slice(part * points + column, part * points + column + LANES)
                        hi, lo = high_low(both[part])
                        hi_b[layer, d, rows, to] = hi
                        lo_b[layer, d, rows, to] = lo

    for layer in range(layers):

        @pl.loop(0, tiles)
        def _(n):
            result = three_products(
                hi_b[layer].reshape(rows_all, 2 * points),
                lo_b[layer].reshape(rows_all, 2 * points),
                table_out[0, n],
                table_out[1, n],
            ).reshape(RADIX, block_rows, width)
            part = n // (tiles // 2)
            first = (n % (tiles // 2)) * (width // x_rows)
            for side in range(width // x_rows):
                for d in range(RADIX):
                    out[(first + side) * RADIX + d, layer, part] = result[
                        d, :, side * x_rows : (side + 1) * x_rows
                    ]


def inverse_y_kernel(recv, table, twiddle, out, high, low, mid):
    count, _, block_rows, x_rows = recv.shape
    sub_rows = block_rows // RADIX
    depth = count * sub_rows

    @pl.loop(0, RADIX)
    def _(v0):
        for part in range(2):
            pieces = [
                recv[k, part, pl.ds(v0, sub_rows, stride=RADIX), :] for k in range(count)
            ]
            turned = jnp.concatenate(pieces, axis=0).T
            hi, lo = high_low(turned)
            high[v0, :, part * depth : (part + 1) * depth] = hi
            low[v0, :, part * depth : (part + 1) * depth] = lo

    tiles, _, width = table.shape[1:]

    @pl.loop(0, tiles)
    def _(n):
        result = three_products(
            high[...].reshape(RADIX * x_rows, 2 * depth),
            low[...].reshape(RADIX * x_rows, 2 * depth),
            table[0, n],
            table[1, n],
        )
        mid[n] = result.reshape(RADIX, x_rows, width)

    trail = out.shape[-1]

    @pl.loop(0, x_rows // 8)
    def _(chunk):
        rows = pl.ds(pl.multiple_of(chunk * 8, 8), 8)
        for lane in range(trail // LANES):
            column = lane * LANES
            lanes = slice(column, column + LANES)
            within = slice(column % width, column % width + LANES)
            tile = column // width
            result = eight_point_to_real(
                [
                    times(
                        (mid[tile, v, rows, within], mid[tile + tiles // 2, v, rows, within]),
                        (twiddle[v, 0:1, lanes], twiddle[v, 1:2, lanes]),
                    )
                    for v in range(RADIX)
                ]
            )
            for s in range(RADIX):
                out[s, rows, lanes] = result[s]


def tile_columns(table, width):
    rows, columns = table.shape
    return table.reshape(rows, columns // width, width).transpose(1, 0, 2)


def vmem_call(kernel, out_shape, scratch, *operands):
    return pl.pallas_call(
        kernel,
        out_shape=jax.ShapeDtypeStruct(out_shape, jnp.float32),
        in_specs=[pl.BlockSpec(memory_space=pltpu.VMEM)] * len(operands),
        out_specs=pl.BlockSpec(memory_space=pltpu.VMEM),
        scratch_shapes=[pltpu.VMEM(shape, dtype) for shape, dtype in scratch],
        compiler_params=pltpu.CompilerParams(vmem_limit_bytes=VMEM_LIMIT),
    )(*operands)


def fast_body(boundary_heat_flux, layer_kernel):
    groups, members = lax.axis_size("grp"), lax.axis_size("dev")
    counts = (groups, members)
    count = groups * members
    local_x, trail = boundary_heat_flux.shape
    x_rows = local_x // members
    layers, _, block_rows, width_x = layer_kernel.shape
    width_y = trail * members
    half = block_rows * count // RADIX
    points = width_x // RADIX
    bf16, f32 = jnp.bfloat16, jnp.float32
    device_pos = lax.axis_index("grp") * members + lax.axis_index("dev")
    first = jnp.logical_and(device_pos == 0, lax.broadcasted_iota(jnp.int32, (block_rows, LANES), 0) == 0)
    weight = jnp.where(first, 1.0, 2.0).astype(f32) * (1.0 / (width_x * width_y))

    table_fy = split_table(complex_table(trail, half, trail, -1.0).T)
    table_in = split_table(tile_columns(complex_table(points, points, points, -1.0), 256))
    table_out = split_table(tile_columns(complex_table(points, points, points, 1.0), 256))
    table_iy = split_table(tile_columns(complex_table(half, trail, trail, 1.0), 256))
    twiddle_fy = twiddle_table(trail, width_y, -1.0)
    twiddle_x = twiddle_table(points, width_x, -1.0)
    twiddle_iy = twiddle_table(trail, width_y, 1.0)

    sent = boundary_heat_flux.reshape(x_rows, members, trail).transpose(1, 0, 2)
    flux = exchange(sent, counts, False, 0)
    spec = vmem_call(
        forward_y_kernel,
        (count, 2, block_rows, x_rows),
        [((RADIX, x_rows, 2 * trail), bf16)] * 2,
        flux,
        table_fy,
        twiddle_fy,
    )
    spec = exchange(spec, counts, True, 1)
    back = vmem_call(
        middle_kernel,
        (count, layers, 2, block_rows, x_rows),
        [((RADIX, block_rows, 2 * points), bf16)] * 2
        + [((2 * points // 256, RADIX, block_rows, 256), f32)]
        + [((layers, RADIX, block_rows, 2 * points), bf16)] * 2,
        spec,
        layer_kernel,
        weight,
        table_in,
        table_out,
        twiddle_x,
    )
    back = exchange(back, counts, True, 2)
    rows = pl.pallas_call(
        inverse_y_kernel,
        grid=(layers,),
        out_shape=jax.ShapeDtypeStruct((members, layers, x_rows, trail), f32),
        in_specs=[
            pl.BlockSpec((count, None, 2, block_rows, x_rows), lambda l: (0, l, 0, 0, 0)),
            pl.BlockSpec(table_iy.shape, lambda l: (0, 0, 0, 0)),
            pl.BlockSpec(twiddle_iy.shape, lambda l: (0, 0, 0)),
        ],
        out_specs=pl.BlockSpec((members, None, x_rows, trail), lambda l: (0, l, 0, 0)),
        scratch_shapes=[
            pltpu.VMEM((RADIX, x_rows, 2 * half), bf16),
            pltpu.VMEM((RADIX, x_rows, 2 * half), bf16),
            pltpu.VMEM((2 * trail // 256, RADIX, x_rows, 256), f32),
        ],
        compiler_params=pltpu.CompilerParams(vmem_limit_bytes=VMEM_LIMIT),
    )(back, table_iy, twiddle_iy)
    rows = exchange(rows, counts, False, 3)
    return rows.transpose(1, 2, 0, 3).reshape(layers, local_x, trail)


def solution(mesh):
    placed = (P("grp", "dev"), P(None, None, ("grp", "dev"), None))
    groups, members = mesh.shape["grp"], mesh.shape["dev"]

    def chosen(boundary_heat_flux, layer_kernel):
        local_x, trail = boundary_heat_flux.shape
        block_rows = layer_kernel.shape[2]
        fits = (
            members == RADIX
            and local_x // members == LANES
            and trail % LANES == 0
            and groups * LANES * RADIX == layer_kernel.shape[3]
            and block_rows % 16 == 0
            and (groups * LANES) % 256 == 0
            and trail % 256 == 0
        )
        return (fast_body if fits else body)(boundary_heat_flux, layer_kernel)

    return jax.shard_map(
        chosen, mesh=mesh, in_specs=placed, out_specs=P(None, "grp", "dev"), check_vma=False
    )
```

```python
import functools
import math

import jax
import jax.numpy as jnp
import numpy as np
from jax import lax
from jax.experimental import pallas as pl
from jax.experimental.pallas import tpu as pltpu
from jax.sharding import PartitionSpec as P


def split_length(length):
    leading = 1
    for candidate in range(1, math.isqrt(length) + 1):
        if length % candidate == 0 and candidate % 2 == 0:
            leading = candidate
    return (leading, length // leading)


def tables(leading, trailing, direction):
    length = leading * trailing
    outer_idx = lax.iota(jnp.int32, leading)
    inner_idx = lax.iota(jnp.int32, trailing)
    angle_outer = (outer_idx[:, None] * outer_idx[None, :] % leading).astype(jnp.float32) * (
        2.0 * math.pi / leading
    )
    angle_twist = (outer_idx[:, None] * inner_idx[None, :] % length).astype(jnp.float32) * (
        2.0 * math.pi / length
    )
    angle_inner = (inner_idx[:, None] * inner_idx[None, :] % trailing).astype(jnp.float32) * (
        2.0 * math.pi / trailing
    )
    return (
        jnp.cos(angle_outer),
        direction * jnp.sin(angle_outer),
        jnp.cos(angle_twist),
        direction * jnp.sin(angle_twist),
        jnp.cos(angle_inner),
        direction * jnp.sin(angle_inner),
    )


def contract(pattern, table, values):
    return jnp.einsum(
        pattern, table, values, precision=lax.Precision.HIGHEST, preferred_element_type=jnp.float32
    )


def section_outer(real_in, imag_in, table, pattern):
    cos_outer, sin_outer, cos_twist, sin_twist = (table[0], table[1], table[2], table[3])
    if imag_in is None:
        real_mid = contract(pattern, cos_outer, real_in)
        imag_mid = contract(pattern, sin_outer, real_in)
    else:
        real_mid = contract(pattern, cos_outer, real_in) - contract(pattern, sin_outer, imag_in)
        imag_mid = contract(pattern, cos_outer, imag_in) + contract(pattern, sin_outer, real_in)
    return (
        real_mid * cos_twist - imag_mid * sin_twist,
        imag_mid * cos_twist + real_mid * sin_twist,
    )


def section_inner(real_mid, imag_mid, table, pattern, real_only):
    cos_inner, sin_inner = (table[4], table[5])
    real_out = contract(pattern, cos_inner, real_mid) - contract(pattern, sin_inner, imag_mid)
    if real_only:
        return real_out
    imag_out = contract(pattern, cos_inner, imag_mid) + contract(pattern, sin_inner, real_mid)
    return (real_out, imag_out)


def reflect_first(values):
    return jnp.roll(jnp.flip(values, -1), 1, -1)


def into_frequency(real_part, imag_part):
    return (
        lax.all_to_all(
            lax.all_to_all(real_part, "grp", split_axis=0, concat_axis=3, tiled=True),
            "dev",
            split_axis=1,
            concat_axis=4,
            tiled=True,
        ),
        lax.all_to_all(
            lax.all_to_all(imag_part, "grp", split_axis=0, concat_axis=3, tiled=True),
            "dev",
            split_axis=1,
            concat_axis=4,
            tiled=True,
        ),
    )


def to_spatial(real_part, imag_part):
    return (
        lax.all_to_all(
            lax.all_to_all(real_part, "grp", split_axis=4, concat_axis=1, tiled=True),
            "dev",
            split_axis=5,
            concat_axis=2,
            tiled=True,
        ),
        lax.all_to_all(
            lax.all_to_all(imag_part, "grp", split_axis=4, concat_axis=1, tiled=True),
            "dev",
            split_axis=5,
            concat_axis=2,
            tiled=True,
        ),
    )


def body(boundary_heat_flux, layer_kernel):
    groups = lax.axis_size("grp")
    members = lax.axis_size("dev")
    columns = lax.all_to_all(boundary_heat_flux, "dev", split_axis=0, concat_axis=1, tiled=True)
    x_rows = columns.shape[0]
    width_y = columns.shape[1]
    width_x = groups * members * x_rows
    half_y = width_y // 2
    block_rows = half_y // (groups * members)
    lead_y, trail_y = split_length(width_y)
    leading_horizontal, trail_x = split_length(width_x)
    ahead_vertical = tables(lead_y, trail_y, -1.0)
    forward_x = tables(leading_horizontal, trail_x, -1.0)
    backward_x = tables(leading_horizontal, trail_x, 1.0)
    backward_y = tables(lead_y, trail_y, 1.0)
    device_pos = lax.axis_index("grp") * members + lax.axis_index("dev")
    first_row = jnp.logical_and(device_pos == 0, lax.iota(jnp.int32, block_rows) == 0)
    first_row = first_row.astype(jnp.float32)[:, None]
    real_mid, imag_mid = section_outer(
        columns.reshape(x_rows, lead_y, trail_y), None, ahead_vertical, "ap,rpq->raq"
    )
    real_spec, imag_spec = section_inner(real_mid, imag_mid, ahead_vertical, "bq,raq->bar", False)
    real_spec = real_spec.reshape(width_y, x_rows)
    imag_spec = imag_spec.reshape(width_y, x_rows)
    lower_shape = (groups, members, block_rows, x_rows)
    sides = 2
    real_remainder = jnp.roll(jnp.flip(real_spec, 0), 1, 0)[:half_y]
    imag_tail = jnp.roll(jnp.flip(imag_spec, 0), 1, 0)[:half_y]
    real_send = jnp.stack(
        [real_spec[:half_y].reshape(lower_shape), real_remainder.reshape(lower_shape)], axis=2
    )
    imag_send = jnp.stack(
        [imag_spec[:half_y].reshape(lower_shape), imag_tail.reshape(lower_shape)], axis=2
    )
    local_rows = sides * block_rows
    shape_sent = (groups, members, local_rows, 1, 1, x_rows)
    real_recv, imag_recv = into_frequency(
        real_send.reshape(shape_sent), imag_send.reshape(shape_sent)
    )
    real_mid, imag_mid = section_outer(
        real_recv.reshape(local_rows, leading_horizontal, trail_x),
        imag_recv.reshape(local_rows, leading_horizontal, trail_x),
        forward_x,
        "ap,rpq->raq",
    )
    real_freq, imag_freq = section_inner(real_mid, imag_mid, forward_x, "bq,raq->rba", False)
    real_freq = real_freq.reshape(local_rows, width_x)
    imag_freq = imag_freq.reshape(local_rows, width_x)
    norm_factor = 1.0 / (width_x * width_y)

    def inverse_x(kernel_pair):
        kernel_real = kernel_pair[0]
        kernel_imag = kernel_pair[1]
        keep_rows = 1.0 - first_row
        kernel_real = jnp.concatenate([kernel_real, reflect_first(kernel_real) * keep_rows], axis=0)
        kernel_imag = jnp.concatenate(
            [kernel_imag, -reflect_first(kernel_imag) * keep_rows], axis=0
        )
        real_prod = real_freq * kernel_real - imag_freq * kernel_imag
        imag_prod = real_freq * kernel_imag + imag_freq * kernel_real
        central_couple = section_outer(
            real_prod.reshape(local_rows, leading_horizontal, trail_x),
            imag_prod.reshape(local_rows, leading_horizontal, trail_x),
            backward_x,
            "ap,rpq->raq",
        )
        real_out, imag_out = section_inner(
            central_couple[0], central_couple[1], backward_x, "bq,raq->rba", False
        )
        real_out = real_out.reshape(local_rows, width_x)
        imag_out = imag_out.reshape(local_rows, width_x)
        shape_back = (1, 1, local_rows, groups, members, x_rows)
        return (real_out.reshape(shape_back), imag_out.reshape(shape_back))

    def inverse_y(real_part, imag_part):
        zero_row = jnp.zeros((1, x_rows), jnp.float32)

        def arrange(values):
            paired = values.reshape(groups * members, 2, block_rows, x_rows)
            lower = paired[:, 0].reshape(half_y, x_rows)
            upper = paired[:, 1].reshape(half_y, x_rows)
            return jnp.concatenate([lower, zero_row, jnp.flip(upper[1:], 0)], axis=0)

        central_couple = section_outer(
            arrange(real_part).reshape(lead_y, trail_y, x_rows),
            arrange(imag_part).reshape(lead_y, trail_y, x_rows),
            backward_y,
            "ap,pqr->raq",
        )
        real_out = section_inner(
            central_couple[0], central_couple[1], backward_y, "bq,raq->rba", True
        )
        return real_out.reshape(x_rows, width_y) * norm_factor

    def finish(kernels):
        real_back, imag_back = jax.vmap(inverse_x)(kernels)
        real_part, imag_part = to_spatial(real_back, imag_back)
        rows_done = jax.vmap(inverse_y)(real_part, imag_part)
        return lax.all_to_all(rows_done, "dev", split_axis=2, concat_axis=1, tiled=True)

    thermal_rise = jnp.concatenate(
        [
            finish(layer_kernel[layer_pos : layer_pos + 1])
            for layer_pos in range(layer_kernel.shape[0])
        ],
        axis=0,
    )
    return thermal_rise


MESH = pl.DeviceIdType.MESH
RADIX = 8
LANES = 128
VMEM_LIMIT = 56 * 1024 * 1024
HALF_ROOT = math.sqrt(0.5)


def high_low(values):
    high = values.astype(jnp.bfloat16)
    return high, (values - high.astype(jnp.float32)).astype(jnp.bfloat16)


def split_table(table):
    table = np.asarray(table, np.float32)
    high = table.astype(jnp.bfloat16)
    low = (table - high.astype(np.float32)).astype(jnp.bfloat16)
    return jnp.asarray(np.stack([high, low]))


def complex_table(rows, columns, length, direction):
    angle = (np.outer(np.arange(rows), np.arange(columns)) % length) * (2.0 * np.pi / length)
    cos, sin = np.cos(angle), direction * np.sin(angle)
    return np.concatenate(
        [np.concatenate([cos, sin], axis=1), np.concatenate([-sin, cos], axis=1)], axis=0
    )


def twiddle_table(points, length, direction):
    angle = (np.outer(np.arange(RADIX), np.arange(points)) % length) * (2.0 * np.pi / length)
    return jnp.asarray(
        np.stack([np.cos(angle), direction * np.sin(angle)], axis=1).astype(np.float32)
    )


def add(a, b):
    return (a[0] + b[0], a[1] + b[1])


def sub(a, b):
    return (a[0] - b[0], a[1] - b[1])


def times(a, b):
    return (a[0] * b[0] - a[1] * b[1], a[0] * b[1] + a[1] * b[0])


def quarter(a, direction):
    return (-a[1], a[0]) if direction > 0 else (a[1], -a[0])


def eighth(a, direction):
    if direction > 0:
        return ((a[0] - a[1]) * HALF_ROOT, (a[0] + a[1]) * HALF_ROOT)
    return ((a[0] + a[1]) * HALF_ROOT, (a[1] - a[0]) * HALF_ROOT)


def four_point(a, direction):
    e0, e1 = add(a[0], a[2]), sub(a[0], a[2])
    o0, o1 = add(a[1], a[3]), quarter(sub(a[1], a[3]), direction)
    return [add(e0, o0), add(e1, o1), sub(e0, o0), sub(e1, o1)]


def eight_point(a, direction):
    even = four_point(a[0::2], direction)
    odd = four_point(a[1::2], direction)
    odd = [
        odd[0],
        eighth(odd[1], direction),
        quarter(odd[2], direction),
        quarter(eighth(odd[3], direction), direction),
    ]
    return [add(e, o) for e, o in zip(even, odd)] + [sub(e, o) for e, o in zip(even, odd)]


def eight_point_of_real(a):
    s0, d0 = a[0] + a[4], a[0] - a[4]
    s1, d1 = a[1] + a[5], a[1] - a[5]
    s2, d2 = a[2] + a[6], a[2] - a[6]
    s3, d3 = a[3] + a[7], a[3] - a[7]
    p, q = (d1 - d3) * HALF_ROOT, (d1 + d3) * HALF_ROOT
    zero = jnp.zeros_like(s0)
    x1 = (d0 + p, -d2 - q)
    x3 = (d0 - p, d2 - q)
    x2 = (s0 - s2, s3 - s1)
    ev, od = s0 + s2, s1 + s3
    conj = lambda z: (z[0], -z[1])
    return [(ev + od, zero), x1, x2, x3, (ev - od, zero), conj(x3), conj(x2), conj(x1)]


def eight_point_to_real(b):
    c1, c2, c3 = [(b[i][0] + b[8 - i][0], b[i][1] - b[8 - i][1]) for i in (1, 2, 3)]
    p, m = b[0][0] + b[4][0], b[0][0] - b[4][0]
    e0, e2 = p + c2[0], p - c2[0]
    e1, e3 = m - c2[1], m + c2[1]
    o0 = c1[0] + c3[0]
    o2 = c3[1] - c1[1]
    o1 = (c1[0] - c1[1] - c3[0] - c3[1]) * HALF_ROOT
    o3 = (c3[0] - c3[1] - c1[0] - c1[1]) * HALF_ROOT
    return [e0 + o0, e1 + o1, e2 + o2, e3 + o3, e0 - o0, e1 - o1, e2 - o2, e3 - o3]


def three_products(high, low, table_high, table_low):
    dot = functools.partial(jnp.dot, preferred_element_type=jnp.float32)
    return dot(high, table_high) + dot(high, table_low) + dot(low, table_high)


PARTS_IN = 4
HALVES = 2


def whole_kernel(
    counts, flux, kernel_hbm, weight_hbm, fy_hbm, in_hbm, out_hbm, iy_hbm, tw_fy_hbm, tw_x_hbm, tw_iy_hbm,
    result_hbm,
    staged, send_rows, recv_rows, high, low, send_spec, recv_spec, hi_a, lo_a, mid_x, hi_b, lo_b,
    send_back, recv_back, mid_y, kernel_ref, weight, table_fy, table_in, table_out, table_iy,
    twiddle_fy, twiddle_x, twiddle_iy,
    load_sem, stage_sem, a_send, a_recv, b_send, b_recv, b_own, c_send, c_recv, c_own, d_send, d_recv, d_own,
    done_sem,
):
    groups, members = counts
    count = groups * members
    grp, dev = lax.axis_index("grp"), lax.axis_index("dev")
    me = grp * members + dev
    layers = kernel_ref.shape[0]
    _, _, x_rows, trail = recv_rows.shape
    part_rows = x_rows // PARTS_IN
    half_rows = recv_spec.shape[3]
    points = groups * x_rows
    lane_blocks = trail // LANES
    sub_rows = HALVES * half_rows // RADIX
    depth = count * sub_rows

    def stage(lane):
        return pltpu.make_async_copy(
            flux.at[:, pl.ds(lane * LANES, LANES)], staged.at[lane], stage_sem.at[lane]
        )

    for lane in range(lane_blocks):
        stage(lane).start()
    loads = [
        pltpu.make_async_copy(a, b, load_sem.at[i])
        for i, (a, b) in enumerate(
            [
                (tw_fy_hbm, twiddle_fy),
                (fy_hbm, table_fy),
                (in_hbm, table_in),
                (kernel_hbm, kernel_ref),
                (weight_hbm, weight),
                (tw_x_hbm, twiddle_x),
                (out_hbm, table_out),
                (iy_hbm, table_iy),
                (tw_iy_hbm, twiddle_iy),
            ]
        )
    ]

    barrier = pltpu.get_barrier_semaphore()

    def place(pos):
        return (lax.div(pos, members), lax.rem(pos, members))

    @pl.loop(1, count)
    def _(offset):
        pl.semaphore_signal(
            barrier, inc=1, device_id=place(lax.rem(me + offset, count)), device_id_type=MESH
        )

    for lane in range(lane_blocks):
        stage(lane).wait()
    for load in loads:
        load.start()
    pl.semaphore_wait(barrier, count - 1)

    for part in range(PARTS_IN):
        rows = pl.ds(part * part_rows, part_rows)

        @pl.loop(1, members)
        def _(offset):
            target = lax.rem(dev + offset, members)
            for lane in range(lane_blocks):
                send_rows[0, target, rows, lane * LANES : (lane + 1) * LANES] = staged[
                    lane, pl.ds(part * part_rows * members + target, part_rows, stride=members), :
                ]
            pltpu.make_async_remote_copy(
                src_ref=send_rows.at[0, target, rows],
                dst_ref=recv_rows.at[0, dev, rows],
                send_sem=a_send.at[part],
                recv_sem=a_recv.at[part],
                device_id=(grp, target),
                device_id_type=MESH,
            ).start()

        for lane in range(lane_blocks):
            recv_rows[0, dev, rows, lane * LANES : (lane + 1) * LANES] = staged[
                lane, pl.ds(part * part_rows * members + dev, part_rows, stride=members), :
            ]

    def wait_bytes(ref, sem):
        pltpu.make_async_copy(ref, ref, sem).wait()

    loads[0].wait()
    for part in range(PARTS_IN):
        wait_bytes(recv_rows.at[0, pl.ds(0, members - 1), pl.ds(part * part_rows, part_rows)], a_recv.at[part])

        @pl.loop(0, part_rows // 16)
        def _(chunk):
            rows = pl.ds(pl.multiple_of(part * part_rows + chunk * 16, 16), 16)
            for lane in range(lane_blocks):
                lanes = slice(lane * LANES, (lane + 1) * LANES)
                parts = eight_point_of_real([recv_rows[0, s, rows, lanes] for s in range(RADIX)])
                for v0 in range(RADIX):
                    pair = times(parts[v0], (twiddle_fy[v0, 0:1, lanes], twiddle_fy[v0, 1:2, lanes]))
                    for side, value in enumerate(pair):
                        to = slice(side * trail + lane * LANES, side * trail + (lane + 1) * LANES)
                        hi, lo = high_low(value)
                        high[v0, rows, to] = hi
                        low[v0, rows, to] = lo

    loads[1].wait()

    def send_all(source, target_of, send_sem, recv_sem, own_sem):
        @pl.loop(1, count)
        def _(offset):
            target = lax.rem(me + offset, count)
            pltpu.make_async_remote_copy(
                src_ref=source.at[target],
                dst_ref=target_of(me),
                send_sem=send_sem,
                recv_sem=recv_sem,
                device_id=place(target),
                device_id_type=MESH,
            ).start()

        pltpu.make_async_copy(source.at[me], target_of(me), own_sem).start()

    def dot_rows(a, b):
        return lax.dot_general(a, b, (((1,), (1,)), ((), ())), preferred_element_type=jnp.float32)

    quarter_rows = half_rows // RADIX
    for half in range(HALVES):

        @pl.loop(0, RADIX // 2)
        def _(pair):
            hi = high[pl.ds(pair * 2, 2)].reshape(2 * x_rows, 2 * trail)
            lo = low[pl.ds(pair * 2, 2)].reshape(2 * x_rows, 2 * trail)
            result = (
                dot_rows(table_fy[0, half], hi)
                + dot_rows(table_fy[1, half], hi)
                + dot_rows(table_fy[0, half], lo)
            )
            for part in range(2):
                for side in range(2):
                    for k in range(count):
                        at = (part * count + k) * quarter_rows
                        send_spec[half, k, part, pl.ds(pair * 2 + side, quarter_rows, stride=RADIX), :] = result[
                            at : at + quarter_rows, side * x_rows : (side + 1) * x_rows
                        ]

        send_all(
            send_spec.at[half], lambda k: recv_spec.at[half, k], b_send.at[half], b_recv.at[half], b_own.at[half]
        )

    tiles, _, width = table_in.shape[1:]
    rows_all = RADIX * half_rows
    for load in loads[2:7]:
        load.wait()
    for half in range(HALVES):
        wait_bytes(recv_spec.at[half, pl.ds(0, count - 1)], b_recv.at[half])
        wait_bytes(recv_spec.at[half, 0], b_own.at[half])

        @pl.loop(0, RADIX)
        def _(d):
            for g in range(groups):
                for part in range(2):
                    to = slice(part * points + g * x_rows, part * points + (g + 1) * x_rows)
                    hi, lo = high_low(recv_spec[half, g * RADIX + d, part])
                    hi_a[d, :, to] = hi
                    lo_a[d, :, to] = lo

        @pl.loop(0, tiles)
        def _(n):
            mid_x[n] = three_products(
                hi_a[...].reshape(rows_all, 2 * points),
                lo_a[...].reshape(rows_all, 2 * points),
                table_in[0, n],
                table_in[1, n],
            ).reshape(RADIX, half_rows, width)

        @pl.loop(0, half_rows // 16)
        def _(chunk):
            rows = pl.ds(pl.multiple_of(chunk * 16, 16), 16)
            rows_of = pl.ds(pl.multiple_of(half * half_rows + chunk * 16, 16), 16)
            scale = weight[rows_of, :]
            for lane in range(points // LANES):
                column = lane * LANES
                lanes = slice(column, column + LANES)
                within = slice(column % width, column % width + LANES)
                tile = column // width
                turn = [(twiddle_x[d, 0:1, lanes], twiddle_x[d, 1:2, lanes]) for d in range(RADIX)]
                spec = eight_point(
                    [
                        times((mid_x[tile, d, rows, within], mid_x[tile + tiles // 2, d, rows, within]), turn[d])
                        for d in range(RADIX)
                    ],
                    -1.0,
                )
                spec = [(a * scale, b * scale) for a, b in spec]
                for layer in range(layers):
                    prod = []
                    for u2 in range(RADIX):
                        at = slice(u2 * points + column, u2 * points + column + LANES)
                        prod.append(
                            times(spec[u2], (kernel_ref[layer, 0, rows_of, at], kernel_ref[layer, 1, rows_of, at]))
                        )
                    back = eight_point(prod, 1.0)
                    for d in range(RADIX):
                        both = times(back[d], (turn[d][0], -turn[d][1]))
                        for part in range(2):
                            to = slice(part * points + column, part * points + column + LANES)
                            hi, lo = high_low(both[part])
                            hi_b[layer, d, rows, to] = hi
                            lo_b[layer, d, rows, to] = lo

        for layer in range(layers):

            @pl.loop(0, tiles)
            def _(n):
                result = three_products(
                    hi_b[layer].reshape(rows_all, 2 * points),
                    lo_b[layer].reshape(rows_all, 2 * points),
                    table_out[0, n],
                    table_out[1, n],
                ).reshape(RADIX, half_rows, width)
                part = n // (tiles // 2)
                first = (n % (tiles // 2)) * (width // x_rows)
                for side in range(width // x_rows):
                    for d in range(RADIX):
                        send_back[half, layer, (first + side) * RADIX + d, part] = result[
                            d, :, side * x_rows : (side + 1) * x_rows
                        ]

            which = half * layers + layer
            span = pl.ds(half * half_rows, half_rows)
            send_all(
                send_back.at[half, layer],
                lambda k: recv_back.at[layer, k, :, span],
                c_send.at[which],
                c_recv.at[which],
                c_own.at[which],
            )

    for part in range(PARTS_IN):
        wait_bytes(send_rows.at[0, pl.ds(0, members - 1), pl.ds(part * part_rows, part_rows)], a_send.at[part])
    for load in loads[7:]:
        load.wait()
    tiles_y, _, width_y = table_iy.shape[1:]

    def rows_copy(layer, offset, source, target):
        return pltpu.make_async_remote_copy(
            src_ref=send_rows.at[layer, target],
            dst_ref=recv_rows.at[layer, source],
            send_sem=d_send.at[layer, offset],
            recv_sem=d_recv.at[layer, offset],
            device_id=(grp, target),
            device_id_type=MESH,
        )

    def rows_own(layer):
        return pltpu.make_async_copy(send_rows.at[layer, dev], recv_rows.at[layer, dev], d_own.at[layer])

    for layer in range(layers):
        for half in range(HALVES):
            which = half * layers + layer
            span = pl.ds(half * half_rows, half_rows)
            wait_bytes(recv_back.at[layer, pl.ds(0, count - 1), :, span], c_recv.at[which])
            wait_bytes(recv_back.at[layer, 0, :, span], c_own.at[which])

        @pl.loop(0, RADIX)
        def _(v0):
            for part in range(2):
                pieces = [
                    recv_back[layer, k, part, pl.ds(v0, sub_rows, stride=RADIX), :] for k in range(count)
                ]
                hi, lo = high_low(jnp.concatenate(pieces, axis=0).T)
                high[v0, :, part * depth : (part + 1) * depth] = hi
                low[v0, :, part * depth : (part + 1) * depth] = lo

        @pl.loop(0, tiles_y)
        def _(n):
            mid_y[n] = three_products(
                high[:, :, : 2 * depth].reshape(RADIX * x_rows, 2 * depth),
                low[:, :, : 2 * depth].reshape(RADIX * x_rows, 2 * depth),
                table_iy[0, n],
                table_iy[1, n],
            ).reshape(RADIX, x_rows, width_y)

        @pl.loop(0, x_rows // 8)
        def _(chunk):
            rows = pl.ds(pl.multiple_of(chunk * 8, 8), 8)
            for lane in range(lane_blocks):
                column = lane * LANES
                lanes = slice(column, column + LANES)
                within = slice(column % width_y, column % width_y + LANES)
                tile = column // width_y
                values = eight_point_to_real(
                    [
                        times(
                            (mid_y[tile, v, rows, within], mid_y[tile + tiles_y // 2, v, rows, within]),
                            (twiddle_iy[v, 0:1, lanes], twiddle_iy[v, 1:2, lanes]),
                        )
                        for v in range(RADIX)
                    ]
                )
                for s in range(RADIX):
                    send_rows[layer, s, rows, lanes] = values[s]

        for offset in range(1, members):
            rows_copy(layer, offset, dev, lax.rem(dev + offset, members)).start()
        rows_own(layer).start()

    def finish(layer, lane):
        return pltpu.make_async_copy(
            staged.at[lane], result_hbm.at[layer, :, pl.ds(lane * LANES, LANES)], done_sem.at[lane]
        )

    for layer in range(layers):
        if layer > 0:
            for lane in range(lane_blocks):
                finish(layer - 1, lane).wait()
        for offset in range(members):
            source = lax.rem(dev + members - offset, members)
            if offset == 0:
                rows_own(layer).wait()
            else:
                rows_copy(layer, offset, source, lax.rem(dev + offset, members)).wait_recv()

            @pl.loop(0, x_rows // 32)
            def _(chunk):
                for lane in range(lane_blocks):
                    staged[lane, pl.ds(chunk * 32 * members + source, 32, stride=members), :] = recv_rows[
                        layer, source, pl.ds(pl.multiple_of(chunk * 32, 32), 32), lane * LANES : (lane + 1) * LANES
                    ]

        for lane in range(lane_blocks):
            finish(layer, lane).start()
    for lane in range(lane_blocks):
        finish(layers - 1, lane).wait()

    for half in range(HALVES):
        wait_bytes(send_spec.at[half, pl.ds(0, count - 1)], b_send.at[half])
        for layer in range(layers):
            wait_bytes(send_back.at[half, layer, pl.ds(0, count - 1)], c_send.at[half * layers + layer])
    for layer in range(layers):
        for offset in range(1, members):
            rows_copy(layer, offset, dev, lax.rem(dev + offset, members)).wait_send()


def tile_columns(table, width):
    rows, columns = table.shape
    return table.reshape(rows, columns // width, width).transpose(1, 0, 2)


def fast_body(boundary_heat_flux, layer_kernel):
    groups, members = lax.axis_size("grp"), lax.axis_size("dev")
    count = groups * members
    local_x, trail = boundary_heat_flux.shape
    x_rows = local_x // members
    layers, _, block_rows, width_x = layer_kernel.shape
    width_y = trail * members
    depth = block_rows * count // RADIX
    points = width_x // RADIX
    half_rows = block_rows // HALVES
    bf16, f32 = jnp.bfloat16, jnp.float32
    device_pos = lax.axis_index("grp") * members + lax.axis_index("dev")
    first = jnp.logical_and(device_pos == 0, lax.broadcasted_iota(jnp.int32, (block_rows, LANES), 0) == 0)
    weight = jnp.where(first, 1.0, 2.0).astype(f32) * (1.0 / (width_x * width_y))

    forward = complex_table(trail, depth, trail, -1.0).T
    forward = forward.reshape(2, count, HALVES, half_rows // RADIX, 2 * trail).transpose(2, 0, 1, 3, 4)
    operands = (
        boundary_heat_flux,
        layer_kernel,
        weight,
        split_table(forward.reshape(HALVES, 2 * depth // HALVES, 2 * trail)),
        split_table(tile_columns(complex_table(points, points, points, -1.0), 256)),
        split_table(tile_columns(complex_table(points, points, points, 1.0), 256)),
        split_table(tile_columns(complex_table(depth, trail, trail, 1.0), 256)),
        twiddle_table(trail, width_y, -1.0),
        twiddle_table(points, width_x, -1.0),
        twiddle_table(trail, width_y, 1.0),
    )
    rows_shape = (layers, members, x_rows, trail)
    buffers = [
        ((trail // LANES, local_x, LANES), f32),
        (rows_shape, f32),
        (rows_shape, f32),
        ((RADIX, x_rows, 2 * trail), bf16),
        ((RADIX, x_rows, 2 * trail), bf16),
        ((HALVES, count, 2, half_rows, x_rows), f32),
        ((HALVES, count, 2, half_rows, x_rows), f32),
        ((RADIX, half_rows, 2 * points), bf16),
        ((RADIX, half_rows, 2 * points), bf16),
        ((2 * points // 256, RADIX, half_rows, 256), f32),
        ((layers, RADIX, half_rows, 2 * points), bf16),
        ((layers, RADIX, half_rows, 2 * points), bf16),
        ((HALVES, layers, count, 2, half_rows, x_rows), f32),
        ((layers, count, 2, block_rows, x_rows), f32),
        ((2 * trail // 256, RADIX, x_rows, 256), f32),
    ] + [(a.shape, a.dtype) for a in operands[1:]]
    dma = lambda *shape: pltpu.SemaphoreType.DMA(shape)
    return pl.pallas_call(
        functools.partial(whole_kernel, (groups, members)),
        out_shape=jax.ShapeDtypeStruct((layers, local_x, trail), f32),
        in_specs=[pl.BlockSpec(memory_space=pl.ANY)] * len(operands),
        out_specs=pl.BlockSpec(memory_space=pl.ANY),
        scratch_shapes=[pltpu.VMEM(shape, dtype) for shape, dtype in buffers]
        + [
            dma(len(operands) - 1),
            dma(trail // LANES),
            dma(PARTS_IN),
            dma(PARTS_IN),
            dma(HALVES),
            dma(HALVES),
            dma(HALVES),
            dma(HALVES * layers),
            dma(HALVES * layers),
            dma(HALVES * layers),
            dma(layers, members),
            dma(layers, members),
            dma(layers),
            dma(trail // LANES),
        ],
        compiler_params=pltpu.CompilerParams(
            collective_id=0, has_side_effects=True, vmem_limit_bytes=VMEM_LIMIT
        ),
    )(*operands)


def solution(mesh):
    placed = (P("grp", "dev"), P(None, None, ("grp", "dev"), None))
    groups, members = mesh.shape["grp"], mesh.shape["dev"]

    def chosen(boundary_heat_flux, layer_kernel):
        local_x, trail = boundary_heat_flux.shape
        block_rows = layer_kernel.shape[2]
        fits = (
            members == RADIX
            and local_x // members == LANES
            and trail % LANES == 0
            and groups * LANES * RADIX == layer_kernel.shape[3]
            and block_rows % (16 * HALVES) == 0
            and (groups * LANES) % 256 == 0
            and trail % 256 == 0
            and block_rows * groups % 32 == 0
        )
        return (fast_body if fits else body)(boundary_heat_flux, layer_kernel)

    return jax.shard_map(
        chosen, mesh=mesh, in_specs=placed, out_specs=P(None, "grp", "dev"), check_vma=False
    )
```

```python
import functools
import math

import jax
import jax.numpy as jnp
import numpy as np
from jax import lax
from jax.experimental import pallas as pl
from jax.experimental.pallas import tpu as pltpu
from jax.sharding import PartitionSpec as P


def split_length(length):
    leading = 1
    for candidate in range(1, math.isqrt(length) + 1):
        if length % candidate == 0 and candidate % 2 == 0:
            leading = candidate
    return (leading, length // leading)


def tables(leading, trailing, direction):
    length = leading * trailing
    outer_idx = lax.iota(jnp.int32, leading)
    inner_idx = lax.iota(jnp.int32, trailing)
    angle_outer = (outer_idx[:, None] * outer_idx[None, :] % leading).astype(jnp.float32) * (
        2.0 * math.pi / leading
    )
    angle_twist = (outer_idx[:, None] * inner_idx[None, :] % length).astype(jnp.float32) * (
        2.0 * math.pi / length
    )
    angle_inner = (inner_idx[:, None] * inner_idx[None, :] % trailing).astype(jnp.float32) * (
        2.0 * math.pi / trailing
    )
    return (
        jnp.cos(angle_outer),
        direction * jnp.sin(angle_outer),
        jnp.cos(angle_twist),
        direction * jnp.sin(angle_twist),
        jnp.cos(angle_inner),
        direction * jnp.sin(angle_inner),
    )


def contract(pattern, table, values):
    return jnp.einsum(
        pattern, table, values, precision=lax.Precision.HIGHEST, preferred_element_type=jnp.float32
    )


def section_outer(real_in, imag_in, table, pattern):
    cos_outer, sin_outer, cos_twist, sin_twist = (table[0], table[1], table[2], table[3])
    if imag_in is None:
        real_mid = contract(pattern, cos_outer, real_in)
        imag_mid = contract(pattern, sin_outer, real_in)
    else:
        real_mid = contract(pattern, cos_outer, real_in) - contract(pattern, sin_outer, imag_in)
        imag_mid = contract(pattern, cos_outer, imag_in) + contract(pattern, sin_outer, real_in)
    return (
        real_mid * cos_twist - imag_mid * sin_twist,
        imag_mid * cos_twist + real_mid * sin_twist,
    )


def section_inner(real_mid, imag_mid, table, pattern, real_only):
    cos_inner, sin_inner = (table[4], table[5])
    real_out = contract(pattern, cos_inner, real_mid) - contract(pattern, sin_inner, imag_mid)
    if real_only:
        return real_out
    imag_out = contract(pattern, cos_inner, imag_mid) + contract(pattern, sin_inner, real_mid)
    return (real_out, imag_out)


def reflect_first(values):
    return jnp.roll(jnp.flip(values, -1), 1, -1)


def into_frequency(real_part, imag_part):
    return (
        lax.all_to_all(
            lax.all_to_all(real_part, "grp", split_axis=0, concat_axis=3, tiled=True),
            "dev",
            split_axis=1,
            concat_axis=4,
            tiled=True,
        ),
        lax.all_to_all(
            lax.all_to_all(imag_part, "grp", split_axis=0, concat_axis=3, tiled=True),
            "dev",
            split_axis=1,
            concat_axis=4,
            tiled=True,
        ),
    )


def to_spatial(real_part, imag_part):
    return (
        lax.all_to_all(
            lax.all_to_all(real_part, "grp", split_axis=4, concat_axis=1, tiled=True),
            "dev",
            split_axis=5,
            concat_axis=2,
            tiled=True,
        ),
        lax.all_to_all(
            lax.all_to_all(imag_part, "grp", split_axis=4, concat_axis=1, tiled=True),
            "dev",
            split_axis=5,
            concat_axis=2,
            tiled=True,
        ),
    )


def body(boundary_heat_flux, layer_kernel):
    groups = lax.axis_size("grp")
    members = lax.axis_size("dev")
    columns = lax.all_to_all(boundary_heat_flux, "dev", split_axis=0, concat_axis=1, tiled=True)
    x_rows = columns.shape[0]
    width_y = columns.shape[1]
    width_x = groups * members * x_rows
    half_y = width_y // 2
    block_rows = half_y // (groups * members)
    lead_y, trail_y = split_length(width_y)
    leading_horizontal, trail_x = split_length(width_x)
    ahead_vertical = tables(lead_y, trail_y, -1.0)
    forward_x = tables(leading_horizontal, trail_x, -1.0)
    backward_x = tables(leading_horizontal, trail_x, 1.0)
    backward_y = tables(lead_y, trail_y, 1.0)
    device_pos = lax.axis_index("grp") * members + lax.axis_index("dev")
    first_row = jnp.logical_and(device_pos == 0, lax.iota(jnp.int32, block_rows) == 0)
    first_row = first_row.astype(jnp.float32)[:, None]
    real_mid, imag_mid = section_outer(
        columns.reshape(x_rows, lead_y, trail_y), None, ahead_vertical, "ap,rpq->raq"
    )
    real_spec, imag_spec = section_inner(real_mid, imag_mid, ahead_vertical, "bq,raq->bar", False)
    real_spec = real_spec.reshape(width_y, x_rows)
    imag_spec = imag_spec.reshape(width_y, x_rows)
    lower_shape = (groups, members, block_rows, x_rows)
    sides = 2
    real_remainder = jnp.roll(jnp.flip(real_spec, 0), 1, 0)[:half_y]
    imag_tail = jnp.roll(jnp.flip(imag_spec, 0), 1, 0)[:half_y]
    real_send = jnp.stack(
        [real_spec[:half_y].reshape(lower_shape), real_remainder.reshape(lower_shape)], axis=2
    )
    imag_send = jnp.stack(
        [imag_spec[:half_y].reshape(lower_shape), imag_tail.reshape(lower_shape)], axis=2
    )
    local_rows = sides * block_rows
    shape_sent = (groups, members, local_rows, 1, 1, x_rows)
    real_recv, imag_recv = into_frequency(
        real_send.reshape(shape_sent), imag_send.reshape(shape_sent)
    )
    real_mid, imag_mid = section_outer(
        real_recv.reshape(local_rows, leading_horizontal, trail_x),
        imag_recv.reshape(local_rows, leading_horizontal, trail_x),
        forward_x,
        "ap,rpq->raq",
    )
    real_freq, imag_freq = section_inner(real_mid, imag_mid, forward_x, "bq,raq->rba", False)
    real_freq = real_freq.reshape(local_rows, width_x)
    imag_freq = imag_freq.reshape(local_rows, width_x)
    norm_factor = 1.0 / (width_x * width_y)

    def inverse_x(kernel_pair):
        kernel_real = kernel_pair[0]
        kernel_imag = kernel_pair[1]
        keep_rows = 1.0 - first_row
        kernel_real = jnp.concatenate([kernel_real, reflect_first(kernel_real) * keep_rows], axis=0)
        kernel_imag = jnp.concatenate(
            [kernel_imag, -reflect_first(kernel_imag) * keep_rows], axis=0
        )
        real_prod = real_freq * kernel_real - imag_freq * kernel_imag
        imag_prod = real_freq * kernel_imag + imag_freq * kernel_real
        central_couple = section_outer(
            real_prod.reshape(local_rows, leading_horizontal, trail_x),
            imag_prod.reshape(local_rows, leading_horizontal, trail_x),
            backward_x,
            "ap,rpq->raq",
        )
        real_out, imag_out = section_inner(
            central_couple[0], central_couple[1], backward_x, "bq,raq->rba", False
        )
        real_out = real_out.reshape(local_rows, width_x)
        imag_out = imag_out.reshape(local_rows, width_x)
        shape_back = (1, 1, local_rows, groups, members, x_rows)
        return (real_out.reshape(shape_back), imag_out.reshape(shape_back))

    def inverse_y(real_part, imag_part):
        zero_row = jnp.zeros((1, x_rows), jnp.float32)

        def arrange(values):
            paired = values.reshape(groups * members, 2, block_rows, x_rows)
            lower = paired[:, 0].reshape(half_y, x_rows)
            upper = paired[:, 1].reshape(half_y, x_rows)
            return jnp.concatenate([lower, zero_row, jnp.flip(upper[1:], 0)], axis=0)

        central_couple = section_outer(
            arrange(real_part).reshape(lead_y, trail_y, x_rows),
            arrange(imag_part).reshape(lead_y, trail_y, x_rows),
            backward_y,
            "ap,pqr->raq",
        )
        real_out = section_inner(
            central_couple[0], central_couple[1], backward_y, "bq,raq->rba", True
        )
        return real_out.reshape(x_rows, width_y) * norm_factor

    def finish(kernels):
        real_back, imag_back = jax.vmap(inverse_x)(kernels)
        real_part, imag_part = to_spatial(real_back, imag_back)
        rows_done = jax.vmap(inverse_y)(real_part, imag_part)
        return lax.all_to_all(rows_done, "dev", split_axis=2, concat_axis=1, tiled=True)

    thermal_rise = jnp.concatenate(
        [
            finish(layer_kernel[layer_pos : layer_pos + 1])
            for layer_pos in range(layer_kernel.shape[0])
        ],
        axis=0,
    )
    return thermal_rise


MESH = pl.DeviceIdType.MESH
RADIX = 8
LANES = 128
VMEM_LIMIT = 56 * 1024 * 1024
HALF_ROOT = math.sqrt(0.5)


def high_low(values):
    high = values.astype(jnp.bfloat16)
    return high, (values - high.astype(jnp.float32)).astype(jnp.bfloat16)


def split_table(table):
    table = np.asarray(table, np.float32)
    high = table.astype(jnp.bfloat16)
    low = (table - high.astype(np.float32)).astype(jnp.bfloat16)
    return jnp.asarray(np.stack([high, low]))


def complex_table(rows, columns, length, direction):
    angle = (np.outer(np.arange(rows), np.arange(columns)) % length) * (2.0 * np.pi / length)
    cos, sin = np.cos(angle), direction * np.sin(angle)
    return np.concatenate(
        [np.concatenate([cos, sin], axis=1), np.concatenate([-sin, cos], axis=1)], axis=0
    )


def twiddle_table(points, length, direction):
    angle = (np.outer(np.arange(RADIX), np.arange(points)) % length) * (2.0 * np.pi / length)
    return jnp.asarray(
        np.stack([np.cos(angle), direction * np.sin(angle)], axis=1).astype(np.float32)
    )


def add(a, b):
    return (a[0] + b[0], a[1] + b[1])


def sub(a, b):
    return (a[0] - b[0], a[1] - b[1])


def times(a, b):
    return (a[0] * b[0] - a[1] * b[1], a[0] * b[1] + a[1] * b[0])


def quarter(a, direction):
    return (-a[1], a[0]) if direction > 0 else (a[1], -a[0])


def eighth(a, direction):
    if direction > 0:
        return ((a[0] - a[1]) * HALF_ROOT, (a[0] + a[1]) * HALF_ROOT)
    return ((a[0] + a[1]) * HALF_ROOT, (a[1] - a[0]) * HALF_ROOT)


def four_point(a, direction):
    e0, e1 = add(a[0], a[2]), sub(a[0], a[2])
    o0, o1 = add(a[1], a[3]), quarter(sub(a[1], a[3]), direction)
    return [add(e0, o0), add(e1, o1), sub(e0, o0), sub(e1, o1)]


def eight_point(a, direction):
    even = four_point(a[0::2], direction)
    odd = four_point(a[1::2], direction)
    odd = [
        odd[0],
        eighth(odd[1], direction),
        quarter(odd[2], direction),
        quarter(eighth(odd[3], direction), direction),
    ]
    return [add(e, o) for e, o in zip(even, odd)] + [sub(e, o) for e, o in zip(even, odd)]


def eight_point_of_real(a):
    s0, d0 = a[0] + a[4], a[0] - a[4]
    s1, d1 = a[1] + a[5], a[1] - a[5]
    s2, d2 = a[2] + a[6], a[2] - a[6]
    s3, d3 = a[3] + a[7], a[3] - a[7]
    p, q = (d1 - d3) * HALF_ROOT, (d1 + d3) * HALF_ROOT
    zero = jnp.zeros_like(s0)
    x1 = (d0 + p, -d2 - q)
    x3 = (d0 - p, d2 - q)
    x2 = (s0 - s2, s3 - s1)
    ev, od = s0 + s2, s1 + s3
    conj = lambda z: (z[0], -z[1])
    return [(ev + od, zero), x1, x2, x3, (ev - od, zero), conj(x3), conj(x2), conj(x1)]


def eight_point_to_real(b):
    c1, c2, c3 = [(b[i][0] + b[8 - i][0], b[i][1] - b[8 - i][1]) for i in (1, 2, 3)]
    p, m = b[0][0] + b[4][0], b[0][0] - b[4][0]
    e0, e2 = p + c2[0], p - c2[0]
    e1, e3 = m - c2[1], m + c2[1]
    o0 = c1[0] + c3[0]
    o2 = c3[1] - c1[1]
    o1 = (c1[0] - c1[1] - c3[0] - c3[1]) * HALF_ROOT
    o3 = (c3[0] - c3[1] - c1[0] - c1[1]) * HALF_ROOT
    return [e0 + o0, e1 + o1, e2 + o2, e3 + o3, e0 - o0, e1 - o1, e2 - o2, e3 - o3]


def three_products(high, low, table_high, table_low):
    dot = functools.partial(jnp.dot, preferred_element_type=jnp.float32)
    return dot(high, table_high) + dot(high, table_low) + dot(low, table_high)


PARTS_IN = 4
HALVES = 2


def whole_kernel(
    counts, flux, kernel_hbm, weight_hbm, fy_hbm, in_hbm, out_hbm, iy_hbm, tw_fy_hbm, tw_x_hbm, tw_iy_hbm,
    result_hbm,
    staged, send_rows, recv_rows, high, low, send_spec, recv_spec, hi_a, lo_a, mid_x, hi_b, lo_b,
    send_back, recv_back, mid_y, kernel_ref, weight, table_fy, table_in, table_out, table_iy,
    twiddle_fy, twiddle_x, twiddle_iy,
    load_sem, stage_sem, a_send, a_recv, b_send, b_recv, b_own, c_send, c_recv, c_own, d_send, d_recv, d_own,
    done_sem,
):
    groups, members = counts
    count = groups * members
    grp, dev = lax.axis_index("grp"), lax.axis_index("dev")
    me = grp * members + dev
    layers = kernel_ref.shape[0]
    _, _, x_rows, trail = recv_rows.shape
    part_rows = x_rows // PARTS_IN
    half_rows = recv_spec.shape[3]
    points = groups * x_rows
    lane_blocks = trail // LANES
    sub_rows = HALVES * half_rows // RADIX
    depth = count * sub_rows

    def stage(lane):
        return pltpu.make_async_copy(
            flux.at[:, pl.ds(lane * LANES, LANES)], staged.at[lane], stage_sem.at[lane]
        )

    for lane in range(lane_blocks):
        stage(lane).start()
    loads = [
        pltpu.make_async_copy(a, b, load_sem.at[i])
        for i, (a, b) in enumerate(
            [
                (tw_fy_hbm, twiddle_fy),
                (fy_hbm, table_fy),
                (in_hbm, table_in),
                (kernel_hbm, kernel_ref),
                (weight_hbm, weight),
                (tw_x_hbm, twiddle_x),
                (out_hbm, table_out),
                (iy_hbm, table_iy),
                (tw_iy_hbm, twiddle_iy),
            ]
        )
    ]

    barrier = pltpu.get_barrier_semaphore()

    def place(pos):
        return (lax.div(pos, members), lax.rem(pos, members))

    @pl.loop(1, count)
    def _(offset):
        pl.semaphore_signal(
            barrier, inc=1, device_id=place(lax.rem(me + offset, count)), device_id_type=MESH
        )

    for lane in range(lane_blocks):
        stage(lane).wait()
    for load in loads:
        load.start()
    pl.semaphore_wait(barrier, count - 1)

    for part in range(PARTS_IN):
        rows = pl.ds(part * part_rows, part_rows)

        @pl.loop(1, members)
        def _(offset):
            target = lax.rem(dev + offset, members)
            for lane in range(lane_blocks):
                send_rows[0, target, rows, lane * LANES : (lane + 1) * LANES] = staged[
                    lane, pl.ds(part * part_rows * members + target, part_rows, stride=members), :
                ]
            pltpu.make_async_remote_copy(
                src_ref=send_rows.at[0, target, rows],
                dst_ref=recv_rows.at[0, dev, rows],
                send_sem=a_send.at[part],
                recv_sem=a_recv.at[part],
                device_id=(grp, target),
                device_id_type=MESH,
            ).start()

        for lane in range(lane_blocks):
            recv_rows[0, dev, rows, lane * LANES : (lane + 1) * LANES] = staged[
                lane, pl.ds(part * part_rows * members + dev, part_rows, stride=members), :
            ]

    def wait_bytes(ref, sem):
        pltpu.make_async_copy(ref, ref, sem).wait()

    loads[0].wait()
    for part in range(PARTS_IN):
        wait_bytes(recv_rows.at[0, pl.ds(0, members - 1), pl.ds(part * part_rows, part_rows)], a_recv.at[part])

        @pl.loop(0, part_rows // 16)
        def _(chunk):
            rows = pl.ds(pl.multiple_of(part * part_rows + chunk * 16, 16), 16)
            for lane in range(lane_blocks):
                lanes = slice(lane * LANES, (lane + 1) * LANES)
                parts = eight_point_of_real([recv_rows[0, s, rows, lanes] for s in range(RADIX)])
                for v0 in range(RADIX):
                    pair = times(parts[v0], (twiddle_fy[v0, 0:1, lanes], twiddle_fy[v0, 1:2, lanes]))
                    for side, value in enumerate(pair):
                        to = slice(side * trail + lane * LANES, side * trail + (lane + 1) * LANES)
                        hi, lo = high_low(value)
                        high[v0, rows, to] = hi
                        low[v0, rows, to] = lo

    loads[1].wait()

    def send_all(source, target_of, send_sem, recv_sem, own_sem):
        @pl.loop(1, count)
        def _(offset):
            target = lax.rem(me + offset, count)
            pltpu.make_async_remote_copy(
                src_ref=source.at[target],
                dst_ref=target_of(me),
                send_sem=send_sem,
                recv_sem=recv_sem,
                device_id=place(target),
                device_id_type=MESH,
            ).start()

        pltpu.make_async_copy(source.at[me], target_of(me), own_sem).start()

    def dot_rows(a, b):
        return lax.dot_general(a, b, (((1,), (1,)), ((), ())), preferred_element_type=jnp.float32)

    quarter_rows = half_rows // RADIX
    for half in range(HALVES):

        @pl.loop(0, RADIX // 2)
        def _(pair):
            hi = high[pl.ds(pair * 2, 2)].reshape(2 * x_rows, 2 * trail)
            lo = low[pl.ds(pair * 2, 2)].reshape(2 * x_rows, 2 * trail)
            result = (
                dot_rows(table_fy[0, half], hi)
                + dot_rows(table_fy[1, half], hi)
                + dot_rows(table_fy[0, half], lo)
            )
            for part in range(2):
                for side in range(2):
                    for k in range(count):
                        at = (part * count + k) * quarter_rows
                        send_spec[half, k, part, pl.ds(pair * 2 + side, quarter_rows, stride=RADIX), :] = result[
                            at : at + quarter_rows, side * x_rows : (side + 1) * x_rows
                        ]

        if half > 0:
            wait_bytes(send_spec.at[half - 1, pl.ds(0, count - 1)], b_send.at[half - 1])
        send_all(
            send_spec.at[half], lambda k: recv_spec.at[half, k], b_send.at[half], b_recv.at[half], b_own.at[half]
        )

    tiles, _, width = table_in.shape[1:]
    rows_all = RADIX * half_rows
    for load in loads[2:7]:
        load.wait()
    for half in range(HALVES):
        wait_bytes(recv_spec.at[half, pl.ds(0, count - 1)], b_recv.at[half])
        wait_bytes(recv_spec.at[half, 0], b_own.at[half])

        @pl.loop(0, RADIX)
        def _(d):
            for g in range(groups):
                for part in range(2):
                    to = slice(part * points + g * x_rows, part * points + (g + 1) * x_rows)
                    hi, lo = high_low(recv_spec[half, g * RADIX + d, part])
                    hi_a[d, :, to] = hi
                    lo_a[d, :, to] = lo

        @pl.loop(0, tiles)
        def _(n):
            mid_x[n] = three_products(
                hi_a[...].reshape(rows_all, 2 * points),
                lo_a[...].reshape(rows_all, 2 * points),
                table_in[0, n],
                table_in[1, n],
            ).reshape(RADIX, half_rows, width)

        @pl.loop(0, half_rows // 16)
        def _(chunk):
            rows = pl.ds(pl.multiple_of(chunk * 16, 16), 16)
            rows_of = pl.ds(pl.multiple_of(half * half_rows + chunk * 16, 16), 16)
            scale = weight[rows_of, :]
            for lane in range(points // LANES):
                column = lane * LANES
                lanes = slice(column, column + LANES)
                within = slice(column % width, column % width + LANES)
                tile = column // width
                turn = [(twiddle_x[d, 0:1, lanes], twiddle_x[d, 1:2, lanes]) for d in range(RADIX)]
                spec = eight_point(
                    [
                        times((mid_x[tile, d, rows, within], mid_x[tile + tiles // 2, d, rows, within]), turn[d])
                        for d in range(RADIX)
                    ],
                    -1.0,
                )
                spec = [(a * scale, b * scale) for a, b in spec]
                for layer in range(layers):
                    prod = []
                    for u2 in range(RADIX):
                        at = slice(u2 * points + column, u2 * points + column + LANES)
                        prod.append(
                            times(spec[u2], (kernel_ref[layer, 0, rows_of, at], kernel_ref[layer, 1, rows_of, at]))
                        )
                    back = eight_point(prod, 1.0)
                    for d in range(RADIX):
                        both = times(back[d], (turn[d][0], -turn[d][1]))
                        for part in range(2):
                            to = slice(part * points + column, part * points + column + LANES)
                            hi, lo = high_low(both[part])
                            hi_b[layer, d, rows, to] = hi
                            lo_b[layer, d, rows, to] = lo

        for layer in range(layers):

            @pl.loop(0, tiles)
            def _(n):
                result = three_products(
                    hi_b[layer].reshape(rows_all, 2 * points),
                    lo_b[layer].reshape(rows_all, 2 * points),
                    table_out[0, n],
                    table_out[1, n],
                ).reshape(RADIX, half_rows, width)
                part = n // (tiles // 2)
                first = (n % (tiles // 2)) * (width // x_rows)
                for side in range(width // x_rows):
                    for d in range(RADIX):
                        send_back[half, layer, (first + side) * RADIX + d, part] = result[
                            d, :, side * x_rows : (side + 1) * x_rows
                        ]

            which = half * layers + layer
            span = pl.ds(half * half_rows, half_rows)
            if half == HALVES - 1 and layer > 0:
                wait_bytes(send_back.at[half, layer - 1, pl.ds(0, count - 1)], c_send.at[which - 1])
            send_all(
                send_back.at[half, layer],
                lambda k: recv_back.at[layer, k, :, span],
                c_send.at[which],
                c_recv.at[which],
                c_own.at[which],
            )

    for part in range(PARTS_IN):
        wait_bytes(send_rows.at[0, pl.ds(0, members - 1), pl.ds(part * part_rows, part_rows)], a_send.at[part])
    for load in loads[7:]:
        load.wait()
    tiles_y, _, width_y = table_iy.shape[1:]

    def rows_copy(layer, offset, source, target):
        return pltpu.make_async_remote_copy(
            src_ref=send_rows.at[layer, target],
            dst_ref=recv_rows.at[layer, source],
            send_sem=d_send.at[layer, offset],
            recv_sem=d_recv.at[layer, offset],
            device_id=(grp, target),
            device_id_type=MESH,
        )

    def rows_own(layer):
        return pltpu.make_async_copy(send_rows.at[layer, dev], recv_rows.at[layer, dev], d_own.at[layer])

    for layer in range(layers):
        for half in range(HALVES):
            which = half * layers + layer
            span = pl.ds(half * half_rows, half_rows)
            wait_bytes(recv_back.at[layer, pl.ds(0, count - 1), :, span], c_recv.at[which])
            wait_bytes(recv_back.at[layer, 0, :, span], c_own.at[which])

        @pl.loop(0, RADIX)
        def _(v0):
            for part in range(2):
                pieces = [
                    recv_back[layer, k, part, pl.ds(v0, sub_rows, stride=RADIX), :] for k in range(count)
                ]
                hi, lo = high_low(jnp.concatenate(pieces, axis=0).T)
                high[v0, :, part * depth : (part + 1) * depth] = hi
                low[v0, :, part * depth : (part + 1) * depth] = lo

        @pl.loop(0, tiles_y)
        def _(n):
            mid_y[n] = three_products(
                high[:, :, : 2 * depth].reshape(RADIX * x_rows, 2 * depth),
                low[:, :, : 2 * depth].reshape(RADIX * x_rows, 2 * depth),
                table_iy[0, n],
                table_iy[1, n],
            ).reshape(RADIX, x_rows, width_y)

        @pl.loop(0, x_rows // 8)
        def _(chunk):
            rows = pl.ds(pl.multiple_of(chunk * 8, 8), 8)
            for lane in range(lane_blocks):
                column = lane * LANES
                lanes = slice(column, column + LANES)
                within = slice(column % width_y, column % width_y + LANES)
                tile = column // width_y
                values = eight_point_to_real(
                    [
                        times(
                            (mid_y[tile, v, rows, within], mid_y[tile + tiles_y // 2, v, rows, within]),
                            (twiddle_iy[v, 0:1, lanes], twiddle_iy[v, 1:2, lanes]),
                        )
                        for v in range(RADIX)
                    ]
                )
                for s in range(RADIX):
                    send_rows[layer, s, rows, lanes] = values[s]

        for offset in range(1, members):
            rows_copy(layer, offset, dev, lax.rem(dev + offset, members)).start()
        rows_own(layer).start()

    def finish(layer, lane):
        return pltpu.make_async_copy(
            staged.at[lane], result_hbm.at[layer, :, pl.ds(lane * LANES, LANES)], done_sem.at[lane]
        )

    for layer in range(layers):
        if layer > 0:
            for lane in range(lane_blocks):
                finish(layer - 1, lane).wait()
        for offset in range(members):
            source = lax.rem(dev + members - offset, members)
            if offset == 0:
                rows_own(layer).wait()
            else:
                rows_copy(layer, offset, source, lax.rem(dev + offset, members)).wait_recv()

            @pl.loop(0, x_rows // 32)
            def _(chunk):
                for lane in range(lane_blocks):
                    staged[lane, pl.ds(chunk * 32 * members + source, 32, stride=members), :] = recv_rows[
                        layer, source, pl.ds(pl.multiple_of(chunk * 32, 32), 32), lane * LANES : (lane + 1) * LANES
                    ]

        for lane in range(lane_blocks):
            finish(layer, lane).start()
    for lane in range(lane_blocks):
        finish(layers - 1, lane).wait()

    for half in range(HALVES):
        for layer in range(layers):
            if half < HALVES - 1 or layer == layers - 1:
                wait_bytes(send_back.at[half, layer, pl.ds(0, count - 1)], c_send.at[half * layers + layer])
    wait_bytes(send_spec.at[HALVES - 1, pl.ds(0, count - 1)], b_send.at[HALVES - 1])
    for layer in range(layers):
        for offset in range(1, members):
            rows_copy(layer, offset, dev, lax.rem(dev + offset, members)).wait_send()


def tile_columns(table, width):
    rows, columns = table.shape
    return table.reshape(rows, columns // width, width).transpose(1, 0, 2)


def fast_body(boundary_heat_flux, layer_kernel):
    groups, members = lax.axis_size("grp"), lax.axis_size("dev")
    count = groups * members
    local_x, trail = boundary_heat_flux.shape
    x_rows = local_x // members
    layers, _, block_rows, width_x = layer_kernel.shape
    width_y = trail * members
    depth = block_rows * count // RADIX
    points = width_x // RADIX
    half_rows = block_rows // HALVES
    bf16, f32 = jnp.bfloat16, jnp.float32
    device_pos = lax.axis_index("grp") * members + lax.axis_index("dev")
    first = jnp.logical_and(device_pos == 0, lax.broadcasted_iota(jnp.int32, (block_rows, LANES), 0) == 0)
    weight = jnp.where(first, 1.0, 2.0).astype(f32) * (1.0 / (width_x * width_y))

    forward = complex_table(trail, depth, trail, -1.0).T
    forward = forward.reshape(2, count, HALVES, half_rows // RADIX, 2 * trail).transpose(2, 0, 1, 3, 4)
    operands = (
        boundary_heat_flux,
        layer_kernel,
        weight,
        split_table(forward.reshape(HALVES, 2 * depth // HALVES, 2 * trail)),
        split_table(tile_columns(complex_table(points, points, points, -1.0), 256)),
        split_table(tile_columns(complex_table(points, points, points, 1.0), 256)),
        split_table(tile_columns(complex_table(depth, trail, trail, 1.0), 256)),
        twiddle_table(trail, width_y, -1.0),
        twiddle_table(points, width_x, -1.0),
        twiddle_table(trail, width_y, 1.0),
    )
    rows_shape = (layers, members, x_rows, trail)
    buffers = [
        ((trail // LANES, local_x, LANES), f32),
        (rows_shape, f32),
        (rows_shape, f32),
        ((RADIX, x_rows, 2 * trail), bf16),
        ((RADIX, x_rows, 2 * trail), bf16),
        ((HALVES, count, 2, half_rows, x_rows), f32),
        ((HALVES, count, 2, half_rows, x_rows), f32),
        ((RADIX, half_rows, 2 * points), bf16),
        ((RADIX, half_rows, 2 * points), bf16),
        ((2 * points // 256, RADIX, half_rows, 256), f32),
        ((layers, RADIX, half_rows, 2 * points), bf16),
        ((layers, RADIX, half_rows, 2 * points), bf16),
        ((HALVES, layers, count, 2, half_rows, x_rows), f32),
        ((layers, count, 2, block_rows, x_rows), f32),
        ((2 * trail // 256, RADIX, x_rows, 256), f32),
    ] + [(a.shape, a.dtype) for a in operands[1:]]
    dma = lambda *shape: pltpu.SemaphoreType.DMA(shape)
    return pl.pallas_call(
        functools.partial(whole_kernel, (groups, members)),
        out_shape=jax.ShapeDtypeStruct((layers, local_x, trail), f32),
        in_specs=[pl.BlockSpec(memory_space=pl.ANY)] * len(operands),
        out_specs=pl.BlockSpec(memory_space=pl.ANY),
        scratch_shapes=[pltpu.VMEM(shape, dtype) for shape, dtype in buffers]
        + [
            dma(len(operands) - 1),
            dma(trail // LANES),
            dma(PARTS_IN),
            dma(PARTS_IN),
            dma(HALVES),
            dma(HALVES),
            dma(HALVES),
            dma(HALVES * layers),
            dma(HALVES * layers),
            dma(HALVES * layers),
            dma(layers, members),
            dma(layers, members),
            dma(layers),
            dma(trail // LANES),
        ],
        compiler_params=pltpu.CompilerParams(
            collective_id=0, has_side_effects=True, vmem_limit_bytes=VMEM_LIMIT
        ),
    )(*operands)


def solution(mesh):
    placed = (P("grp", "dev"), P(None, None, ("grp", "dev"), None))
    groups, members = mesh.shape["grp"], mesh.shape["dev"]

    def chosen(boundary_heat_flux, layer_kernel):
        local_x, trail = boundary_heat_flux.shape
        block_rows = layer_kernel.shape[2]
        fits = (
            members == RADIX
            and local_x // members == LANES
            and trail % LANES == 0
            and groups * LANES * RADIX == layer_kernel.shape[3]
            and block_rows % (16 * HALVES) == 0
            and (groups * LANES) % 256 == 0
            and trail % 256 == 0
            and block_rows * groups % 32 == 0
        )
        return (fast_body if fits else body)(boundary_heat_flux, layer_kernel)

    return jax.shard_map(
        chosen, mesh=mesh, in_specs=placed, out_specs=P(None, "grp", "dev"), check_vma=False
    )
```

```python
import functools
import math

import jax
import jax.numpy as jnp
import numpy as np
from jax import lax
from jax.experimental import pallas as pl
from jax.experimental.pallas import tpu as pltpu
from jax.sharding import PartitionSpec as P


def split_length(length):
    leading = 1
    for candidate in range(1, math.isqrt(length) + 1):
        if length % candidate == 0 and candidate % 2 == 0:
            leading = candidate
    return (leading, length // leading)


def tables(leading, trailing, direction):
    length = leading * trailing
    outer_idx = lax.iota(jnp.int32, leading)
    inner_idx = lax.iota(jnp.int32, trailing)
    angle_outer = (outer_idx[:, None] * outer_idx[None, :] % leading).astype(jnp.float32) * (
        2.0 * math.pi / leading
    )
    angle_twist = (outer_idx[:, None] * inner_idx[None, :] % length).astype(jnp.float32) * (
        2.0 * math.pi / length
    )
    angle_inner = (inner_idx[:, None] * inner_idx[None, :] % trailing).astype(jnp.float32) * (
        2.0 * math.pi / trailing
    )
    return (
        jnp.cos(angle_outer),
        direction * jnp.sin(angle_outer),
        jnp.cos(angle_twist),
        direction * jnp.sin(angle_twist),
        jnp.cos(angle_inner),
        direction * jnp.sin(angle_inner),
    )


def contract(pattern, table, values):
    return jnp.einsum(
        pattern, table, values, precision=lax.Precision.HIGHEST, preferred_element_type=jnp.float32
    )


def section_outer(real_in, imag_in, table, pattern):
    cos_outer, sin_outer, cos_twist, sin_twist = (table[0], table[1], table[2], table[3])
    if imag_in is None:
        real_mid = contract(pattern, cos_outer, real_in)
        imag_mid = contract(pattern, sin_outer, real_in)
    else:
        real_mid = contract(pattern, cos_outer, real_in) - contract(pattern, sin_outer, imag_in)
        imag_mid = contract(pattern, cos_outer, imag_in) + contract(pattern, sin_outer, real_in)
    return (
        real_mid * cos_twist - imag_mid * sin_twist,
        imag_mid * cos_twist + real_mid * sin_twist,
    )


def section_inner(real_mid, imag_mid, table, pattern, real_only):
    cos_inner, sin_inner = (table[4], table[5])
    real_out = contract(pattern, cos_inner, real_mid) - contract(pattern, sin_inner, imag_mid)
    if real_only:
        return real_out
    imag_out = contract(pattern, cos_inner, imag_mid) + contract(pattern, sin_inner, real_mid)
    return (real_out, imag_out)


def reflect_first(values):
    return jnp.roll(jnp.flip(values, -1), 1, -1)


def into_frequency(real_part, imag_part):
    return (
        lax.all_to_all(
            lax.all_to_all(real_part, "grp", split_axis=0, concat_axis=3, tiled=True),
            "dev",
            split_axis=1,
            concat_axis=4,
            tiled=True,
        ),
        lax.all_to_all(
            lax.all_to_all(imag_part, "grp", split_axis=0, concat_axis=3, tiled=True),
            "dev",
            split_axis=1,
            concat_axis=4,
            tiled=True,
        ),
    )


def to_spatial(real_part, imag_part):
    return (
        lax.all_to_all(
            lax.all_to_all(real_part, "grp", split_axis=4, concat_axis=1, tiled=True),
            "dev",
            split_axis=5,
            concat_axis=2,
            tiled=True,
        ),
        lax.all_to_all(
            lax.all_to_all(imag_part, "grp", split_axis=4, concat_axis=1, tiled=True),
            "dev",
            split_axis=5,
            concat_axis=2,
            tiled=True,
        ),
    )


def body(boundary_heat_flux, layer_kernel):
    groups = lax.axis_size("grp")
    members = lax.axis_size("dev")
    columns = lax.all_to_all(boundary_heat_flux, "dev", split_axis=0, concat_axis=1, tiled=True)
    x_rows = columns.shape[0]
    width_y = columns.shape[1]
    width_x = groups * members * x_rows
    half_y = width_y // 2
    block_rows = half_y // (groups * members)
    lead_y, trail_y = split_length(width_y)
    leading_horizontal, trail_x = split_length(width_x)
    ahead_vertical = tables(lead_y, trail_y, -1.0)
    forward_x = tables(leading_horizontal, trail_x, -1.0)
    backward_x = tables(leading_horizontal, trail_x, 1.0)
    backward_y = tables(lead_y, trail_y, 1.0)
    device_pos = lax.axis_index("grp") * members + lax.axis_index("dev")
    first_row = jnp.logical_and(device_pos == 0, lax.iota(jnp.int32, block_rows) == 0)
    first_row = first_row.astype(jnp.float32)[:, None]
    real_mid, imag_mid = section_outer(
        columns.reshape(x_rows, lead_y, trail_y), None, ahead_vertical, "ap,rpq->raq"
    )
    real_spec, imag_spec = section_inner(real_mid, imag_mid, ahead_vertical, "bq,raq->bar", False)
    real_spec = real_spec.reshape(width_y, x_rows)
    imag_spec = imag_spec.reshape(width_y, x_rows)
    lower_shape = (groups, members, block_rows, x_rows)
    sides = 2
    real_remainder = jnp.roll(jnp.flip(real_spec, 0), 1, 0)[:half_y]
    imag_tail = jnp.roll(jnp.flip(imag_spec, 0), 1, 0)[:half_y]
    real_send = jnp.stack(
        [real_spec[:half_y].reshape(lower_shape), real_remainder.reshape(lower_shape)], axis=2
    )
    imag_send = jnp.stack(
        [imag_spec[:half_y].reshape(lower_shape), imag_tail.reshape(lower_shape)], axis=2
    )
    local_rows = sides * block_rows
    shape_sent = (groups, members, local_rows, 1, 1, x_rows)
    real_recv, imag_recv = into_frequency(
        real_send.reshape(shape_sent), imag_send.reshape(shape_sent)
    )
    real_mid, imag_mid = section_outer(
        real_recv.reshape(local_rows, leading_horizontal, trail_x),
        imag_recv.reshape(local_rows, leading_horizontal, trail_x),
        forward_x,
        "ap,rpq->raq",
    )
    real_freq, imag_freq = section_inner(real_mid, imag_mid, forward_x, "bq,raq->rba", False)
    real_freq = real_freq.reshape(local_rows, width_x)
    imag_freq = imag_freq.reshape(local_rows, width_x)
    norm_factor = 1.0 / (width_x * width_y)

    def inverse_x(kernel_pair):
        kernel_real = kernel_pair[0]
        kernel_imag = kernel_pair[1]
        keep_rows = 1.0 - first_row
        kernel_real = jnp.concatenate([kernel_real, reflect_first(kernel_real) * keep_rows], axis=0)
        kernel_imag = jnp.concatenate(
            [kernel_imag, -reflect_first(kernel_imag) * keep_rows], axis=0
        )
        real_prod = real_freq * kernel_real - imag_freq * kernel_imag
        imag_prod = real_freq * kernel_imag + imag_freq * kernel_real
        central_couple = section_outer(
            real_prod.reshape(local_rows, leading_horizontal, trail_x),
            imag_prod.reshape(local_rows, leading_horizontal, trail_x),
            backward_x,
            "ap,rpq->raq",
        )
        real_out, imag_out = section_inner(
            central_couple[0], central_couple[1], backward_x, "bq,raq->rba", False
        )
        real_out = real_out.reshape(local_rows, width_x)
        imag_out = imag_out.reshape(local_rows, width_x)
        shape_back = (1, 1, local_rows, groups, members, x_rows)
        return (real_out.reshape(shape_back), imag_out.reshape(shape_back))

    def inverse_y(real_part, imag_part):
        zero_row = jnp.zeros((1, x_rows), jnp.float32)

        def arrange(values):
            paired = values.reshape(groups * members, 2, block_rows, x_rows)
            lower = paired[:, 0].reshape(half_y, x_rows)
            upper = paired[:, 1].reshape(half_y, x_rows)
            return jnp.concatenate([lower, zero_row, jnp.flip(upper[1:], 0)], axis=0)

        central_couple = section_outer(
            arrange(real_part).reshape(lead_y, trail_y, x_rows),
            arrange(imag_part).reshape(lead_y, trail_y, x_rows),
            backward_y,
            "ap,pqr->raq",
        )
        real_out = section_inner(
            central_couple[0], central_couple[1], backward_y, "bq,raq->rba", True
        )
        return real_out.reshape(x_rows, width_y) * norm_factor

    def finish(kernels):
        real_back, imag_back = jax.vmap(inverse_x)(kernels)
        real_part, imag_part = to_spatial(real_back, imag_back)
        rows_done = jax.vmap(inverse_y)(real_part, imag_part)
        return lax.all_to_all(rows_done, "dev", split_axis=2, concat_axis=1, tiled=True)

    thermal_rise = jnp.concatenate(
        [
            finish(layer_kernel[layer_pos : layer_pos + 1])
            for layer_pos in range(layer_kernel.shape[0])
        ],
        axis=0,
    )
    return thermal_rise


MESH = pl.DeviceIdType.MESH
RADIX = 8
LANES = 128
VMEM_LIMIT = 56 * 1024 * 1024
HALF_ROOT = math.sqrt(0.5)


def high_low(values):
    high = values.astype(jnp.bfloat16)
    return high, (values - high.astype(jnp.float32)).astype(jnp.bfloat16)


def split_table(table):
    table = np.asarray(table, np.float32)
    high = table.astype(jnp.bfloat16)
    low = (table - high.astype(np.float32)).astype(jnp.bfloat16)
    return jnp.asarray(np.stack([high, low]))


def complex_table(rows, columns, length, direction):
    angle = (np.outer(np.arange(rows), np.arange(columns)) % length) * (2.0 * np.pi / length)
    cos, sin = np.cos(angle), direction * np.sin(angle)
    return np.concatenate(
        [np.concatenate([cos, sin], axis=1), np.concatenate([-sin, cos], axis=1)], axis=0
    )


def twiddle_table(points, length, direction):
    angle = (np.outer(np.arange(RADIX), np.arange(points)) % length) * (2.0 * np.pi / length)
    return jnp.asarray(
        np.stack([np.cos(angle), direction * np.sin(angle)], axis=1).astype(np.float32)
    )


def add(a, b):
    return (a[0] + b[0], a[1] + b[1])


def sub(a, b):
    return (a[0] - b[0], a[1] - b[1])


def times(a, b):
    return (a[0] * b[0] - a[1] * b[1], a[0] * b[1] + a[1] * b[0])


def quarter(a, direction):
    return (-a[1], a[0]) if direction > 0 else (a[1], -a[0])


def eighth(a, direction):
    if direction > 0:
        return ((a[0] - a[1]) * HALF_ROOT, (a[0] + a[1]) * HALF_ROOT)
    return ((a[0] + a[1]) * HALF_ROOT, (a[1] - a[0]) * HALF_ROOT)


def four_point(a, direction):
    e0, e1 = add(a[0], a[2]), sub(a[0], a[2])
    o0, o1 = add(a[1], a[3]), quarter(sub(a[1], a[3]), direction)
    return [add(e0, o0), add(e1, o1), sub(e0, o0), sub(e1, o1)]


def eight_point(a, direction):
    even = four_point(a[0::2], direction)
    odd = four_point(a[1::2], direction)
    odd = [
        odd[0],
        eighth(odd[1], direction),
        quarter(odd[2], direction),
        quarter(eighth(odd[3], direction), direction),
    ]
    return [add(e, o) for e, o in zip(even, odd)] + [sub(e, o) for e, o in zip(even, odd)]


def eight_point_of_real(a):
    s0, d0 = a[0] + a[4], a[0] - a[4]
    s1, d1 = a[1] + a[5], a[1] - a[5]
    s2, d2 = a[2] + a[6], a[2] - a[6]
    s3, d3 = a[3] + a[7], a[3] - a[7]
    p, q = (d1 - d3) * HALF_ROOT, (d1 + d3) * HALF_ROOT
    zero = jnp.zeros_like(s0)
    x1 = (d0 + p, -d2 - q)
    x3 = (d0 - p, d2 - q)
    x2 = (s0 - s2, s3 - s1)
    ev, od = s0 + s2, s1 + s3
    conj = lambda z: (z[0], -z[1])
    return [(ev + od, zero), x1, x2, x3, (ev - od, zero), conj(x3), conj(x2), conj(x1)]


def eight_point_to_real(b):
    c1, c2, c3 = [(b[i][0] + b[8 - i][0], b[i][1] - b[8 - i][1]) for i in (1, 2, 3)]
    p, m = b[0][0] + b[4][0], b[0][0] - b[4][0]
    e0, e2 = p + c2[0], p - c2[0]
    e1, e3 = m - c2[1], m + c2[1]
    o0 = c1[0] + c3[0]
    o2 = c3[1] - c1[1]
    o1 = (c1[0] - c1[1] - c3[0] - c3[1]) * HALF_ROOT
    o3 = (c3[0] - c3[1] - c1[0] - c1[1]) * HALF_ROOT
    return [e0 + o0, e1 + o1, e2 + o2, e3 + o3, e0 - o0, e1 - o1, e2 - o2, e3 - o3]


def three_products(high, low, table_high, table_low):
    dot = functools.partial(jnp.dot, preferred_element_type=jnp.float32)
    return dot(high, table_high) + dot(high, table_low) + dot(low, table_high)


PARTS_IN = 8
HALVES = 2


def whole_kernel(
    counts, flux, kernel_hbm, weight_hbm, fy_hbm, in_hbm, out_hbm, iy_hbm, tw_fy_hbm, tw_x_hbm, tw_iy_hbm,
    result_hbm,
    staged, send_rows, recv_rows, high, low, send_spec, recv_spec, hi_a, lo_a, mid_x, hi_b, lo_b,
    send_back, recv_back, mid_y, kernel_ref, weight, table_fy, table_in, table_out, table_iy,
    twiddle_fy, twiddle_x, twiddle_iy,
    load_sem, stage_sem, a_send, a_recv, b_send, b_recv, b_own, c_send, c_recv, c_own, d_send, d_recv, d_own,
    done_sem,
):
    groups, members = counts
    count = groups * members
    grp, dev = lax.axis_index("grp"), lax.axis_index("dev")
    me = grp * members + dev
    layers = kernel_ref.shape[0]
    _, _, x_rows, trail = recv_rows.shape
    part_rows = x_rows // PARTS_IN
    half_rows = recv_spec.shape[3]
    points = groups * x_rows
    lane_blocks = trail // LANES
    sub_rows = HALVES * half_rows // RADIX
    depth = count * sub_rows

    def stage(lane):
        return pltpu.make_async_copy(
            flux.at[:, pl.ds(lane * LANES, LANES)], staged.at[lane], stage_sem.at[lane]
        )

    for lane in range(lane_blocks):
        stage(lane).start()
    loads = [
        pltpu.make_async_copy(a, b, load_sem.at[i])
        for i, (a, b) in enumerate(
            [
                (tw_fy_hbm, twiddle_fy),
                (fy_hbm, table_fy),
                (in_hbm, table_in),
                (kernel_hbm, kernel_ref),
                (weight_hbm, weight),
                (tw_x_hbm, twiddle_x),
                (out_hbm, table_out),
                (iy_hbm, table_iy),
                (tw_iy_hbm, twiddle_iy),
            ]
        )
    ]

    barrier = pltpu.get_barrier_semaphore()

    def place(pos):
        return (lax.div(pos, members), lax.rem(pos, members))

    @pl.loop(1, count)
    def _(offset):
        pl.semaphore_signal(
            barrier, inc=1, device_id=place(lax.rem(me + offset, count)), device_id_type=MESH
        )

    for lane in range(lane_blocks):
        stage(lane).wait()
    for load in loads:
        load.start()
    pl.semaphore_wait(barrier, count - 1)

    for part in range(PARTS_IN):
        rows = pl.ds(part * part_rows, part_rows)

        @pl.loop(1, members)
        def _(offset):
            target = lax.rem(dev + offset, members)
            for lane in range(lane_blocks):
                send_rows[0, target, rows, lane * LANES : (lane + 1) * LANES] = staged[
                    lane, pl.ds(part * part_rows * members + target, part_rows, stride=members), :
                ]
            pltpu.make_async_remote_copy(
                src_ref=send_rows.at[0, target, rows],
                dst_ref=recv_rows.at[0, dev, rows],
                send_sem=a_send.at[part],
                recv_sem=a_recv.at[part],
                device_id=(grp, target),
                device_id_type=MESH,
            ).start()

        for lane in range(lane_blocks):
            recv_rows[0, dev, rows, lane * LANES : (lane + 1) * LANES] = staged[
                lane, pl.ds(part * part_rows * members + dev, part_rows, stride=members), :
            ]

    def wait_bytes(ref, sem):
        pltpu.make_async_copy(ref, ref, sem).wait()

    loads[0].wait()
    for part in range(PARTS_IN):
        wait_bytes(recv_rows.at[0, pl.ds(0, members - 1), pl.ds(part * part_rows, part_rows)], a_recv.at[part])

        @pl.loop(0, part_rows // 16)
        def _(chunk):
            rows = pl.ds(pl.multiple_of(part * part_rows + chunk * 16, 16), 16)
            for lane in range(lane_blocks):
                lanes = slice(lane * LANES, (lane + 1) * LANES)
                parts = eight_point_of_real([recv_rows[0, s, rows, lanes] for s in range(RADIX)])
                for v0 in range(RADIX):
                    pair = times(parts[v0], (twiddle_fy[v0, 0:1, lanes], twiddle_fy[v0, 1:2, lanes]))
                    for side, value in enumerate(pair):
                        to = slice(side * trail + lane * LANES, side * trail + (lane + 1) * LANES)
                        hi, lo = high_low(value)
                        high[v0, rows, to] = hi
                        low[v0, rows, to] = lo

    loads[1].wait()

    def send_all(source, target_of, send_sem, recv_sem, own_sem):
        @pl.loop(1, count)
        def _(offset):
            target = lax.rem(me + offset, count)
            pltpu.make_async_remote_copy(
                src_ref=source.at[target],
                dst_ref=target_of(me),
                send_sem=send_sem,
                recv_sem=recv_sem,
                device_id=place(target),
                device_id_type=MESH,
            ).start()

        pltpu.make_async_copy(source.at[me], target_of(me), own_sem).start()

    def dot_rows(a, b):
        return lax.dot_general(a, b, (((1,), (1,)), ((), ())), preferred_element_type=jnp.float32)

    quarter_rows = half_rows // RADIX
    for half in range(HALVES):

        @pl.loop(0, RADIX // 2)
        def _(pair):
            hi = high[pl.ds(pair * 2, 2)].reshape(2 * x_rows, 2 * trail)
            lo = low[pl.ds(pair * 2, 2)].reshape(2 * x_rows, 2 * trail)
            result = (
                dot_rows(table_fy[0, half], hi)
                + dot_rows(table_fy[1, half], hi)
                + dot_rows(table_fy[0, half], lo)
            )
            for part in range(2):
                for side in range(2):
                    for k in range(count):
                        at = (part * count + k) * quarter_rows
                        send_spec[half, k, part, pl.ds(pair * 2 + side, quarter_rows, stride=RADIX), :] = result[
                            at : at + quarter_rows, side * x_rows : (side + 1) * x_rows
                        ]

        send_all(
            send_spec.at[half], lambda k: recv_spec.at[half, k], b_send.at[half], b_recv.at[half], b_own.at[half]
        )

    tiles, _, width = table_in.shape[1:]
    rows_all = RADIX * half_rows
    for load in loads[2:7]:
        load.wait()
    for half in range(HALVES):
        wait_bytes(recv_spec.at[half, pl.ds(0, count - 1)], b_recv.at[half])
        wait_bytes(recv_spec.at[half, 0], b_own.at[half])

        @pl.loop(0, RADIX)
        def _(d):
            for g in range(groups):
                for part in range(2):
                    to = slice(part * points + g * x_rows, part * points + (g + 1) * x_rows)
                    hi, lo = high_low(recv_spec[half, g * RADIX + d, part])
                    hi_a[d, :, to] = hi
                    lo_a[d, :, to] = lo

        @pl.loop(0, tiles)
        def _(n):
            mid_x[n] = three_products(
                hi_a[...].reshape(rows_all, 2 * points),
                lo_a[...].reshape(rows_all, 2 * points),
                table_in[0, n],
                table_in[1, n],
            ).reshape(RADIX, half_rows, width)

        @pl.loop(0, half_rows // 16)
        def _(chunk):
            rows = pl.ds(pl.multiple_of(chunk * 16, 16), 16)
            rows_of = pl.ds(pl.multiple_of(half * half_rows + chunk * 16, 16), 16)
            scale = weight[rows_of, :]
            for lane in range(points // LANES):
                column = lane * LANES
                lanes = slice(column, column + LANES)
                within = slice(column % width, column % width + LANES)
                tile = column // width
                turn = [(twiddle_x[d, 0:1, lanes], twiddle_x[d, 1:2, lanes]) for d in range(RADIX)]
                spec = eight_point(
                    [
                        times((mid_x[tile, d, rows, within], mid_x[tile + tiles // 2, d, rows, within]), turn[d])
                        for d in range(RADIX)
                    ],
                    -1.0,
                )
                spec = [(a * scale, b * scale) for a, b in spec]
                for layer in range(layers):
                    prod = []
                    for u2 in range(RADIX):
                        at = slice(u2 * points + column, u2 * points + column + LANES)
                        prod.append(
                            times(spec[u2], (kernel_ref[layer, 0, rows_of, at], kernel_ref[layer, 1, rows_of, at]))
                        )
                    back = eight_point(prod, 1.0)
                    for d in range(RADIX):
                        both = times(back[d], (turn[d][0], -turn[d][1]))
                        for part in range(2):
                            to = slice(part * points + column, part * points + column + LANES)
                            hi, lo = high_low(both[part])
                            hi_b[layer, d, rows, to] = hi
                            lo_b[layer, d, rows, to] = lo

        for layer in range(layers):

            @pl.loop(0, tiles)
            def _(n):
                result = three_products(
                    hi_b[layer].reshape(rows_all, 2 * points),
                    lo_b[layer].reshape(rows_all, 2 * points),
                    table_out[0, n],
                    table_out[1, n],
                ).reshape(RADIX, half_rows, width)
                part = n // (tiles // 2)
                first = (n % (tiles // 2)) * (width // x_rows)
                for side in range(width // x_rows):
                    for d in range(RADIX):
                        send_back[half, layer, (first + side) * RADIX + d, part] = result[
                            d, :, side * x_rows : (side + 1) * x_rows
                        ]

            which = half * layers + layer
            span = pl.ds(half * half_rows, half_rows)
            send_all(
                send_back.at[half, layer],
                lambda k: recv_back.at[layer, k, :, span],
                c_send.at[which],
                c_recv.at[which],
                c_own.at[which],
            )

    for part in range(PARTS_IN):
        wait_bytes(send_rows.at[0, pl.ds(0, members - 1), pl.ds(part * part_rows, part_rows)], a_send.at[part])
    for load in loads[7:]:
        load.wait()
    tiles_y, _, width_y = table_iy.shape[1:]

    def rows_copy(layer, offset, source, target):
        return pltpu.make_async_remote_copy(
            src_ref=send_rows.at[layer, target],
            dst_ref=recv_rows.at[layer, source],
            send_sem=d_send.at[layer, offset],
            recv_sem=d_recv.at[layer, offset],
            device_id=(grp, target),
            device_id_type=MESH,
        )

    def rows_own(layer):
        return pltpu.make_async_copy(send_rows.at[layer, dev], recv_rows.at[layer, dev], d_own.at[layer])

    for layer in range(layers):
        for half in range(HALVES):
            which = half * layers + layer
            span = pl.ds(half * half_rows, half_rows)
            wait_bytes(recv_back.at[layer, pl.ds(0, count - 1), :, span], c_recv.at[which])
            wait_bytes(recv_back.at[layer, 0, :, span], c_own.at[which])

        @pl.loop(0, RADIX)
        def _(v0):
            for part in range(2):
                pieces = [
                    recv_back[layer, k, part, pl.ds(v0, sub_rows, stride=RADIX), :] for k in range(count)
                ]
                hi, lo = high_low(jnp.concatenate(pieces, axis=0).T)
                high[v0, :, part * depth : (part + 1) * depth] = hi
                low[v0, :, part * depth : (part + 1) * depth] = lo

        @pl.loop(0, tiles_y)
        def _(n):
            mid_y[n] = three_products(
                high[:, :, : 2 * depth].reshape(RADIX * x_rows, 2 * depth),
                low[:, :, : 2 * depth].reshape(RADIX * x_rows, 2 * depth),
                table_iy[0, n],
                table_iy[1, n],
            ).reshape(RADIX, x_rows, width_y)

        @pl.loop(0, x_rows // 8)
        def _(chunk):
            rows = pl.ds(pl.multiple_of(chunk * 8, 8), 8)
            for lane in range(lane_blocks):
                column = lane * LANES
                lanes = slice(column, column + LANES)
                within = slice(column % width_y, column % width_y + LANES)
                tile = column // width_y
                values = eight_point_to_real(
                    [
                        times(
                            (mid_y[tile, v, rows, within], mid_y[tile + tiles_y // 2, v, rows, within]),
                            (twiddle_iy[v, 0:1, lanes], twiddle_iy[v, 1:2, lanes]),
                        )
                        for v in range(RADIX)
                    ]
                )
                for s in range(RADIX):
                    send_rows[layer, s, rows, lanes] = values[s]

        for offset in range(1, members):
            rows_copy(layer, offset, dev, lax.rem(dev + offset, members)).start()
        rows_own(layer).start()

    def finish(layer, lane):
        return pltpu.make_async_copy(
            staged.at[lane], result_hbm.at[layer, :, pl.ds(lane * LANES, LANES)], done_sem.at[lane]
        )

    for layer in range(layers):
        if layer > 0:
            for lane in range(lane_blocks):
                finish(layer - 1, lane).wait()
        for offset in range(members):
            source = lax.rem(dev + members - offset, members)
            if offset == 0:
                rows_own(layer).wait()
            else:
                rows_copy(layer, offset, source, lax.rem(dev + offset, members)).wait_recv()

            @pl.loop(0, x_rows // 32)
            def _(chunk):
                for lane in range(lane_blocks):
                    staged[lane, pl.ds(chunk * 32 * members + source, 32, stride=members), :] = recv_rows[
                        layer, source, pl.ds(pl.multiple_of(chunk * 32, 32), 32), lane * LANES : (lane + 1) * LANES
                    ]

        for lane in range(lane_blocks):
            finish(layer, lane).start()
    for lane in range(lane_blocks):
        finish(layers - 1, lane).wait()

    for half in range(HALVES):
        wait_bytes(send_spec.at[half, pl.ds(0, count - 1)], b_send.at[half])
        for layer in range(layers):
            wait_bytes(send_back.at[half, layer, pl.ds(0, count - 1)], c_send.at[half * layers + layer])
    for layer in range(layers):
        for offset in range(1, members):
            rows_copy(layer, offset, dev, lax.rem(dev + offset, members)).wait_send()


def tile_columns(table, width):
    rows, columns = table.shape
    return table.reshape(rows, columns // width, width).transpose(1, 0, 2)


def fast_body(boundary_heat_flux, layer_kernel):
    groups, members = lax.axis_size("grp"), lax.axis_size("dev")
    count = groups * members
    local_x, trail = boundary_heat_flux.shape
    x_rows = local_x // members
    layers, _, block_rows, width_x = layer_kernel.shape
    width_y = trail * members
    depth = block_rows * count // RADIX
    points = width_x // RADIX
    half_rows = block_rows // HALVES
    bf16, f32 = jnp.bfloat16, jnp.float32
    device_pos = lax.axis_index("grp") * members + lax.axis_index("dev")
    first = jnp.logical_and(device_pos == 0, lax.broadcasted_iota(jnp.int32, (block_rows, LANES), 0) == 0)
    weight = jnp.where(first, 1.0, 2.0).astype(f32) * (1.0 / (width_x * width_y))

    forward = complex_table(trail, depth, trail, -1.0).T
    forward = forward.reshape(2, count, HALVES, half_rows // RADIX, 2 * trail).transpose(2, 0, 1, 3, 4)
    operands = (
        boundary_heat_flux,
        layer_kernel,
        weight,
        split_table(forward.reshape(HALVES, 2 * depth // HALVES, 2 * trail)),
        split_table(tile_columns(complex_table(points, points, points, -1.0), 256)),
        split_table(tile_columns(complex_table(points, points, points, 1.0), 256)),
        split_table(tile_columns(complex_table(depth, trail, trail, 1.0), 256)),
        twiddle_table(trail, width_y, -1.0),
        twiddle_table(points, width_x, -1.0),
        twiddle_table(trail, width_y, 1.0),
    )
    rows_shape = (layers, members, x_rows, trail)
    buffers = [
        ((trail // LANES, local_x, LANES), f32),
        (rows_shape, f32),
        (rows_shape, f32),
        ((RADIX, x_rows, 2 * trail), bf16),
        ((RADIX, x_rows, 2 * trail), bf16),
        ((HALVES, count, 2, half_rows, x_rows), f32),
        ((HALVES, count, 2, half_rows, x_rows), f32),
        ((RADIX, half_rows, 2 * points), bf16),
        ((RADIX, half_rows, 2 * points), bf16),
        ((2 * points // 256, RADIX, half_rows, 256), f32),
        ((layers, RADIX, half_rows, 2 * points), bf16),
        ((layers, RADIX, half_rows, 2 * points), bf16),
        ((HALVES, layers, count, 2, half_rows, x_rows), f32),
        ((layers, count, 2, block_rows, x_rows), f32),
        ((2 * trail // 256, RADIX, x_rows, 256), f32),
    ] + [(a.shape, a.dtype) for a in operands[1:]]
    dma = lambda *shape: pltpu.SemaphoreType.DMA(shape)
    return pl.pallas_call(
        functools.partial(whole_kernel, (groups, members)),
        out_shape=jax.ShapeDtypeStruct((layers, local_x, trail), f32),
        in_specs=[pl.BlockSpec(memory_space=pl.ANY)] * len(operands),
        out_specs=pl.BlockSpec(memory_space=pl.ANY),
        scratch_shapes=[pltpu.VMEM(shape, dtype) for shape, dtype in buffers]
        + [
            dma(len(operands) - 1),
            dma(trail // LANES),
            dma(PARTS_IN),
            dma(PARTS_IN),
            dma(HALVES),
            dma(HALVES),
            dma(HALVES),
            dma(HALVES * layers),
            dma(HALVES * layers),
            dma(HALVES * layers),
            dma(layers, members),
            dma(layers, members),
            dma(layers),
            dma(trail // LANES),
        ],
        compiler_params=pltpu.CompilerParams(
            collective_id=0, has_side_effects=True, vmem_limit_bytes=VMEM_LIMIT
        ),
    )(*operands)


def solution(mesh):
    placed = (P("grp", "dev"), P(None, None, ("grp", "dev"), None))
    groups, members = mesh.shape["grp"], mesh.shape["dev"]

    def chosen(boundary_heat_flux, layer_kernel):
        local_x, trail = boundary_heat_flux.shape
        block_rows = layer_kernel.shape[2]
        fits = (
            members == RADIX
            and local_x // members == LANES
            and trail % LANES == 0
            and groups * LANES * RADIX == layer_kernel.shape[3]
            and block_rows % (16 * HALVES) == 0
            and (groups * LANES) % 256 == 0
            and trail % 256 == 0
            and block_rows * groups % 32 == 0
        )
        return (fast_body if fits else body)(boundary_heat_flux, layer_kernel)

    return jax.shard_map(
        chosen, mesh=mesh, in_specs=placed, out_specs=P(None, "grp", "dev"), check_vma=False
    )
```
